32 devices in a mesh: clips: 2 (over y), frame: 4 (over z), row: 2 (over x), head: 2 (over core).
Axes of the slice: x: 2, y: 2, z: 4, core: 2. Of those that a mesh axis runs over, the one named last changes fastest.
Arguments:
- query: bfloat16 [64, 16, 8, 1536], P(('clips', 'frame'), 'row', None, 'head'), parts along dimension 0, may hold values from -7 to 7
- keys: bfloat16 [64, 16, 8, 1536], P(('clips', 'frame'), 'row', None, 'head'), parts along dimension 0, may hold values from -6 to 6
- values: bfloat16 [64, 16, 8, 1536], P(('clips', 'frame'), 'row', None, 'head'), parts along dimension 0, may hold values from -6 to 6
Outputs:
- attended: bfloat16 [64, 16, 8, 1536], P(('clips', 'frame'), 'row', None, 'head'), parts along dimension 0
The draws below stay inside these ranges and needn't reach their ends.
There are 2 independent parts, one for each index of `clips`. The reference program is written for one: setup_inputs(seed, part) draws one part's arguments, and reference() takes and returns one part's arrays. A program takes and returns all parts, laid end to end along the dimension named above; each array names one. Nothing has to cross between parts.
All inputs are finite; a program needn't handle non-finite values.
Results may differ from the reference program's by a relative error of at most 0.0047.
Values may be sent and summed in bfloat16 or wider, within the bound.
No kernel may reach another device: no remote copies, remote signals or barrier semaphores. Data moves between devices by JAX's collectives and lax.ppermute only.
A program may use at most 64 MiB of HBM per device.

```python
import math
import jax
import jax.numpy as jnp
from jax import lax

HEADS = 12
HD = 128
TF = 4
TR = 8
TC = 8
LATENT_FRAMES = 32
ROWS = 16
COLS = 8


def draw_query(key, part):
    full_shape = (LATENT_FRAMES, ROWS, COLS, HEADS * HD)
    result_values = jnp.clip(jax.random.normal(jax.random.fold_in(key, 21), full_shape, jnp.float32), -6.0, 6.0)
    return result_values.astype(jnp.bfloat16)


def draw_keys(key, part):
    full_shape = (LATENT_FRAMES, ROWS, COLS, HEADS * HD)
    result_values = jnp.clip(jax.random.normal(jax.random.fold_in(key, 31), full_shape, jnp.float32), -6.0, 6.0)
    return result_values.astype(jnp.bfloat16)


def shard_levels(own_key, shape, split, least, largest):
    loudness = 1.0
    for dim, parts in split:
        heights = jax.random.uniform(jax.random.fold_in(jax.random.fold_in(own_key, 6), dim), (parts,), jnp.float32, least / len(split), largest / len(split))
        loudness = loudness * jnp.repeat(jnp.exp(heights), shape[dim] // parts).reshape((-1,) + (1,) * (len(shape) - 1 - dim))
    return loudness


def noise(own_key, extent, width, bound, shards=(), kind=jnp.bfloat16):
    values = jax.random.normal(own_key, extent, jnp.float32) * width
    if len(shards) > 0:
        values = shard_levels(own_key, extent, shards, -0.22, 0.18) * values
    return jnp.clip(values, min=-bound, max=bound).astype(kind)


def setup_inputs(seed: int = 0, part: int = 0) -> dict:
    arg_keys = jax.random.split(jax.random.key(seed), 4)
    part_splits = jax.random.split(jax.random.fold_in(arg_keys[3], part), 4)
    return {
        "query": draw_query(jax.random.fold_in(jax.random.fold_in(arg_keys[3], part), 71), part),
        "keys": draw_keys(jax.random.fold_in(jax.random.fold_in(arg_keys[3], part), 71), part),
        "values": noise(part_splits[2], (LATENT_FRAMES, ROWS, COLS, HEADS * HD), 1.0, 6.0, ((0, 4), (1, 2), (3, 2))),
    }


def reference(query, keys, values):
    frames, rows, columns, features = query.shape
    heads = features // HD
    frame_tiles = frames // TF
    row_tiles = rows // TR
    column_tiles = columns // TC
    tile_size = TF * TR * TC
    score_scale = 1.0 / math.sqrt(HD)

    def tiled(array):
        shaped = array.reshape(frame_tiles, TF, row_tiles, TR, column_tiles, TC, heads, HD)
        shaped = shaped.transpose(0, 2, 4, 1, 3, 5, 6, 7)
        return shaped.reshape(frame_tiles, row_tiles, column_tiles, tile_size, heads, HD)
    padding = ((1, 1), (1, 1), (0, 0), (0, 0), (0, 0), (0, 0))
    tiled_queries = tiled(query)
    key_tiles = jnp.pad(tiled(keys), padding)
    value_tiles = jnp.pad(tiled(values), padding)
    offsets = jnp.arange(3, dtype=jnp.int32) - 1
    block_rows = column_tiles * tile_size

    def one_tile(flat):
        frame_at = (flat // row_tiles).astype(jnp.int32)
        row_at = (flat % row_tiles).astype(jnp.int32)
        zero = jnp.zeros((), jnp.int32)
        starts = (frame_at, row_at, zero, zero, zero, zero)
        query_block = lax.dynamic_slice(tiled_queries, starts, (1, 1, column_tiles, tile_size, heads, HD))
        key_block = lax.dynamic_slice(key_tiles, starts, (3, 3, column_tiles, tile_size, heads, HD))
        value_block = lax.dynamic_slice(value_tiles, starts, (3, 3, column_tiles, tile_size, heads, HD))
        frame_ids = frame_at + offsets
        row_ids = row_at + offsets
        frame_ok = (frame_ids >= 0) & (frame_ids < frame_tiles)
        row_ok = (row_ids >= 0) & (row_ids < row_tiles)
        tile_mask = frame_ok[:, None] & row_ok[None, :]
        allowed = jnp.broadcast_to(tile_mask[None, :, :, None], (block_rows, 3, 3, block_rows))
        allowed = allowed.reshape(block_rows, 9 * block_rows)
        queries = query_block.reshape(block_rows, heads, HD).astype(jnp.float32)
        key_rows = key_block.reshape(-1, heads, HD).astype(jnp.float32)
        value_rows = value_block.reshape(-1, heads, HD).astype(jnp.float32)
        scores = jnp.einsum('qhd,khd->hqk', queries, key_rows) * score_scale
        scores = jnp.where(allowed[None], scores, -jnp.inf)
        row_peak = lax.optimization_barrier(jnp.max(scores, axis=-1, keepdims=True))
        weights = jnp.exp(scores - row_peak)
        row_total = lax.optimization_barrier(jnp.sum(weights, axis=-1, keepdims=True))
        rounded_length = lax.optimization_barrier(weights.astype(jnp.bfloat16)).astype(jnp.float32)
        summed = jnp.einsum('hqk,khd->qhd', rounded_length, value_rows)
        return (summed / jnp.transpose(row_total, (1, 0, 2))).astype(jnp.bfloat16)
    results = lax.map(one_tile, jnp.arange(frame_tiles * row_tiles, dtype=jnp.int32))
    results = results.reshape(frame_tiles, row_tiles, column_tiles, TF, TR, TC, heads, HD)
    results = results.transpose(0, 3, 1, 4, 2, 5, 6, 7)
    return results.reshape(frames, rows, columns, features)
```

```python
import functools
import math

import jax
import jax.numpy as jnp
from jax import lax
from jax.experimental import pallas as pl
from jax.experimental.pallas import tpu as pltpu
from jax.sharding import PartitionSpec as P

HD = 128
TF = 4
TR = 8
TC = 8
TILE = TF * TR * TC
ROWS = 2 * TILE
EXPONENT = math.log2(math.e) / math.sqrt(HD)
NT = (((1,), (1,)), ((), ()))
NN = (((1,), (0,)), ((), ()))
STAT_ROWS = 3 * 8 * ROWS // HD
CHUNKS = (2, 4)


def dot(a, b, dims):
    return lax.dot_general(a, b, dims, preferred_element_type=jnp.float32)


def attend(q, k, v, before, after):
    place = lax.axis_index("frame")
    present = (place > 0, place < lax.axis_size("frame") - 1)
    outs, logs = [], []
    for t, side in enumerate((before, after)):
        qt = q[t * TILE : (t + 1) * TILE]
        k_side = jnp.where(present[t], side[:TILE], k[:TILE])
        v_side = side[TILE:]
        s_own = dot(qt, k, NT)
        s_side = dot(qt, k_side, NT)
        peak = jnp.maximum(
            jnp.max(s_own, axis=1, keepdims=True), jnp.max(s_side, axis=1, keepdims=True)
        )
        w_own = jnp.exp2((s_own - peak) * EXPONENT)
        w_side = jnp.exp2((s_side - peak) * EXPONENT)
        counted = jnp.where(present[t], 1.0, 0.0)
        total = jnp.sum(w_own, axis=1, keepdims=True) + counted * jnp.sum(
            w_side, axis=1, keepdims=True
        )
        summed = dot(w_own.astype(jnp.bfloat16), v, NN) + dot(
            w_side.astype(jnp.bfloat16), v_side, NN
        )
        outs.append(summed * (1.0 / total))
        logs.append(peak * EXPONENT + jnp.log2(total))
    return jnp.concatenate(outs, 0), jnp.concatenate(logs, 0)


def put_column(ref, j, column):
    lanes = lax.broadcasted_iota(jnp.int32, ref.shape, 1)
    ref[...] = jnp.where(lanes == j, column, ref[...])


def pack_logs(logs):
    flat = logs.T[:8]
    parts = []
    for _ in range(3):
        part = flat.astype(jnp.bfloat16).astype(jnp.float32)
        flat = flat - part
        parts += [part[:, i : i + HD] for i in range(0, ROWS, HD)]
    return jnp.concatenate(parts, 0).astype(jnp.bfloat16)


def unpack_logs(packed):
    parts = packed.astype(jnp.float32)
    third = STAT_ROWS // 3
    flat = parts[:third] + parts[third : 2 * third] + parts[2 * third :]
    flat = jnp.concatenate([flat[i : i + 8] for i in range(0, third, 8)], 1)
    return jnp.concatenate([flat, jnp.zeros((HD - 8, ROWS), jnp.float32)], 0).T


def remote_kernel(heads, q, k, v, before, after, out, logs):
    j = pl.program_id(0)

    @pl.when(j == 0)
    def _():
        logs[...] = jnp.zeros_like(logs)

    o, log = attend(q[...], k[...], v[...], before[...], after[...])
    out[pl.ds(pl.multiple_of(j * ROWS, ROWS), ROWS), :] = o.astype(out.dtype)
    put_column(logs, j, log)

    @pl.when(j == heads - 1)
    def _():
        out[heads * ROWS :, :] = pack_logs(logs[...])


def local_kernel(splits, q, k, v, *rest):
    sides, (out, logs) = rest[:-2], rest[-2:]
    j = pl.program_id(0)

    @pl.when(j == 0)
    def _():
        logs[...] = jnp.zeros_like(logs)

    start = 0
    for c, heads in enumerate(splits):
        @pl.when((j >= start) & (j < start + heads))
        def _(c=c):
            o, log = attend(q[...], k[...], v[...], sides[2 * c][...], sides[2 * c + 1][...])
            out[...] = o
            put_column(logs, j, log)

        start += heads


def combine_kernel(first, heads, groups, own, logs, *rest):
    theirs, out, columns = rest[:groups], rest[-2], rest[-1]
    j = pl.program_id(0)
    place = lax.axis_index("row")
    if groups == 1:
        there = (None,)
    else:
        there = (place < lax.axis_size("row") - 1, place > 0)

    @pl.when(j == 0)
    def _():
        for g in range(groups):
            got = unpack_logs(theirs[g][heads * ROWS :, :])
            if there[g] is not None:
                got = jnp.where(there[g], got, -jnp.inf)
            columns[g] = got

    lanes = lax.broadcasted_iota(jnp.int32, (ROWS, HD), 1)

    def column(block, at):
        return jnp.sum(jnp.where(lanes == at, block, 0.0), axis=1, keepdims=True)

    own_log = column(logs[...], first + j)
    their_logs = [column(columns[g], j) for g in range(groups)]
    top = functools.reduce(jnp.maximum, their_logs, own_log)
    weight = jnp.exp2(own_log - top)
    total = weight
    summed = weight * own[...]
    for g in range(groups):
        weight = jnp.exp2(their_logs[g] - top)
        total = total + weight
        block = theirs[g][pl.ds(pl.multiple_of(j * ROWS, ROWS), ROWS), :]
        summed = summed + weight * block.astype(jnp.float32)
    out[...] = (summed * (1.0 / total)).astype(out.dtype)


def cost(heads, tiles=6):
    pairs = heads * tiles * TILE * TILE
    return pl.CostEstimate(flops=4 * pairs * HD, bytes_accessed=heads * 8 * ROWS * HD, transcendentals=pairs)


def head_block(shift=0):
    return pl.BlockSpec((ROWS, HD), lambda j: (0, j + shift))


def whole_block(shape):
    return pl.BlockSpec(shape, lambda j: (0,) * len(shape))


def remote_part(first, heads, q, k, v, before, after):
    shape = (heads * ROWS + STAT_ROWS, HD)
    return pl.pallas_call(
        functools.partial(remote_kernel, heads),
        grid=(heads,),
        in_specs=[head_block(), head_block(first), head_block(first), head_block(), head_block()],
        out_specs=whole_block(shape),
        out_shape=jax.ShapeDtypeStruct(shape, jnp.bfloat16),
        scratch_shapes=[pltpu.VMEM((ROWS, HD), jnp.float32)],
        compiler_params=pltpu.CompilerParams(vmem_limit_bytes=32 * 1024 * 1024),
        cost_estimate=cost(heads),
        name="remote_part",
    )(q, k, v, before, after)


def local_part(splits, q, k, v, sides):
    heads = sum(splits)
    specs, start = [], 0
    for count in splits:
        spec = pl.BlockSpec(
            (ROWS, HD), lambda j, s=start, n=count: (0, jnp.clip(j - s, 0, n - 1))
        )
        specs += [spec, spec]
        start += count
    return pl.pallas_call(
        functools.partial(local_kernel, splits),
        grid=(heads,),
        in_specs=[head_block()] * 3 + specs,
        out_specs=[head_block(), whole_block((ROWS, HD))],
        out_shape=[
            jax.ShapeDtypeStruct((ROWS, heads * HD), jnp.float32),
            jax.ShapeDtypeStruct((ROWS, HD), jnp.float32),
        ],
        compiler_params=pltpu.CompilerParams(vmem_limit_bytes=32 * 1024 * 1024),
        cost_estimate=cost(heads),
        name="local_part",
    )(q, k, v, *sides)


def combine_part(first, heads, own, logs, theirs, width, prior):
    groups = len(theirs)
    specs = [head_block(first), whole_block((ROWS, HD))] + [whole_block(t.shape) for t in theirs]
    operands = [own, logs, *theirs]
    aliases = {}
    if prior is not None:
        specs.append(pl.BlockSpec(memory_space=pl.ANY))
        aliases = {len(operands): 0}
        operands.append(prior)
    return pl.pallas_call(
        functools.partial(combine_kernel, first, heads, groups),
        grid=(heads,),
        in_specs=specs,
        out_specs=head_block(first),
        out_shape=jax.ShapeDtypeStruct((ROWS, width), jnp.bfloat16),
        scratch_shapes=[pltpu.VMEM((groups, ROWS, HD), jnp.float32)],
        input_output_aliases=aliases,
        compiler_params=pltpu.CompilerParams(vmem_limit_bytes=32 * 1024 * 1024),
        cost_estimate=pl.CostEstimate(
            flops=8 * heads * ROWS * HD, bytes_accessed=heads * 8 * ROWS * HD, transcendentals=0
        ),
        name="combine_part",
    )(*operands)


def per_device(query, keys, values):
    features = query.shape[3]
    heads = features // HD
    splits = CHUNKS if sum(CHUNKS) == heads else (heads,)
    q = query.reshape(ROWS, features)
    k = keys.reshape(ROWS, features)
    v = values.reshape(ROWS, features)
    frames = lax.axis_size("frame")
    rows = lax.axis_size("row")
    later = [(i, i + 1) for i in range(frames - 1)]
    sooner = [(i + 1, i) for i in range(frames - 1)]
    if rows == 2:
        routes = [([(0, 1), (1, 0)], [(0, 1), (1, 0)])]
    else:
        down = [(i, i + 1) for i in range(rows - 1)]
        up = [(i + 1, i) for i in range(rows - 1)]
        routes = [(down, up), (up, down)]

    bounds, start = [], 0
    for count in splits:
        bounds.append((start, start + count))
        start += count

    got_q, sides = [], []
    for a, b in bounds:
        a, b = a * HD, b * HD
        got_q.append([lax.ppermute(q[:, a:b], "row", there) for there, _ in routes])
        tail = jnp.concatenate([k[TILE:, a:b], v[TILE:, a:b]], 0)
        head = jnp.concatenate([k[:TILE, a:b], v[:TILE, a:b]], 0)
        sides.append((lax.ppermute(tail, "frame", later), lax.ppermute(head, "frame", sooner)))

    answers = []
    for (a, b), chunk_q, (before, after) in zip(bounds, got_q, sides):
        parts = [remote_part(a, b - a, one, k, v, before, after) for one in chunk_q]
        answers.append(parts)

    q_local, _ = lax.optimization_barrier((q, answers[-1]))
    own, logs = local_part(splits, q_local, k, v, [s for pair in sides for s in pair])

    out = None
    for (a, b), parts in zip(bounds, answers):
        theirs = [lax.ppermute(p, "row", back) for p, (_, back) in zip(parts, routes)]
        out = combine_part(a, b - a, own, logs, theirs, features, out)
    return out.reshape(query.shape)


def solution(mesh):
    spec = P(("clips", "frame"), "row", None, "head")
    return jax.shard_map(
        per_device, mesh=mesh, in_specs=(spec,) * 3, out_specs=spec, check_vma=False
    )
```

```python
import functools
import math

import jax
import jax.numpy as jnp
from jax import lax
from jax.experimental import pallas as pl
from jax.experimental.pallas import tpu as pltpu
from jax.sharding import PartitionSpec as P

HD = 128
TF = 4
TR = 8
TC = 8
TILE = TF * TR * TC
ROWS = 2 * TILE
EXPONENT = math.log2(math.e) / math.sqrt(HD)
NT = (((1,), (1,)), ((), ()))
NN = (((1,), (0,)), ((), ()))
BLOCKS = ROWS // HD
LOG_ROWS = 16
CHUNKS = (3, 3)
VMEM_BYTES = 48 * 1024 * 1024


def dot(a, b, dims):
    return lax.dot_general(a, b, dims, preferred_element_type=jnp.float32)


def attend(first, heads, q, k, v, even, odd, store):
    place = lax.axis_index("frame")
    present = (place > 0, place < lax.axis_size("frame") - 1)
    is_even = lax.rem(place, 2) == 0
    ones = jnp.ones((ROWS, HD), jnp.bfloat16)
    lanes = lax.broadcasted_iota(jnp.int32, (HD, HD), 1)
    logs = jnp.zeros((HD, HD), jnp.float32)
    for t in range(2):
        rows = slice(t * TILE, (t + 1) * TILE)
        near, far = (odd, even) if t == 0 else (even, odd)
        for j in range(heads):
            here = slice(j * HD, (j + 1) * HD)
            own = slice((first + j) * HD, (first + j + 1) * HD)
            q_tile = q[rows, here]
            k_own = k[:, own]
            v_own = jnp.concatenate([v[:, own], ones], 1)
            side = jnp.where(is_even, near[:, here], far[:, here])
            k_side = jnp.where(present[t], side[:TILE], k_own[:TILE])
            v_side = jnp.concatenate([side[TILE:], ones[:TILE]], 1)
            v_side = jnp.where(present[t], v_side, jnp.zeros_like(v_side))
            s_own = dot(q_tile, k_own, NT)
            s_side = dot(q_tile, k_side, NT)
            peak = jnp.maximum(
                jnp.max(s_own, axis=1, keepdims=True), jnp.max(s_side, axis=1, keepdims=True)
            )
            w_own = jnp.exp2((s_own - peak) * EXPONENT).astype(jnp.bfloat16)
            w_side = jnp.exp2((s_side - peak) * EXPONENT).astype(jnp.bfloat16)
            summed = dot(w_own, v_own, NN) + dot(w_side, v_side, NN)
            total = summed[:, HD:]
            store(rows, here, summed[:, :HD] / total)
            log = peak * EXPONENT + jnp.log2(total[:, :1])
            for i in range(TILE // HD):
                at = (t * (TILE // HD) + i) * (LOG_ROWS // BLOCKS) + j
                logs = jnp.where(lanes == at, log[i * HD : (i + 1) * HD], logs)
    return logs


def pack_logs(logs):
    flat = logs.T[:LOG_ROWS]
    parts = []
    for _ in range(3):
        part = flat.astype(jnp.bfloat16)
        flat = flat - part.astype(jnp.float32)
        parts.append(part)
    return jnp.concatenate(parts, 1)


def unpack_logs(packed):
    parts = packed.astype(jnp.float32)
    flat = parts[:, :HD] + parts[:, HD : 2 * HD] + parts[:, 2 * HD :]
    return jnp.concatenate([flat, jnp.zeros((HD - LOG_ROWS, HD), jnp.float32)], 0).T


def remote_kernel(first, heads, q, k, v, even, odd, out):
    def store(rows, here, block):
        out[rows, here] = block.astype(out.dtype)

    logs = attend(first, heads, q, k, v, even, odd, store)
    out[ROWS:, :] = pack_logs(logs)


def local_kernel(splits, q, k, v, *rest):
    sides, (out, logs) = rest[:-2], rest[-2:]
    first = 0
    for c, heads in enumerate(splits):
        columns = slice(first * HD, (first + heads) * HD)

        def store(rows, here, block, first=first):
            out[rows, first * HD + here.start : first * HD + here.stop] = block

        logs[c] = attend(
            first, heads, q.at[:, columns], k, v, sides[2 * c], sides[2 * c + 1], store
        )
        first += heads


def combine_kernel(chunk, heads, groups, own, logs, *rest):
    theirs, out = rest[:groups], rest[-1]
    place = lax.axis_index("row")
    if groups == 1:
        there = (None,)
    else:
        there = (place < lax.axis_size("row") - 1, place > 0)
    all_logs = [logs[0]]
    for g in range(groups):
        got = unpack_logs(theirs[g][ROWS:, :])
        if there[g] is not None:
            got = jnp.where(there[g], got, -jnp.inf)
        all_logs.append(got)
    top = functools.reduce(jnp.maximum, all_logs)
    weights = [jnp.exp2(x - top) for x in all_logs]
    total = functools.reduce(jnp.add, weights)
    shares = [w / total for w in weights]
    for b in range(BLOCKS):
        rows = slice(b * HD, (b + 1) * HD)
        for j in range(heads):
            here = slice(j * HD, (j + 1) * HD)
            at = b * (LOG_ROWS // BLOCKS) + j
            summed = shares[0][:, at : at + 1] * own[rows, here]
            for g in range(groups):
                block = theirs[g][rows, here].astype(jnp.float32)
                summed = summed + shares[g + 1][:, at : at + 1] * block
            out[rows, here] = summed.astype(out.dtype)


def cost(heads, tiles=6):
    pairs = heads * tiles * TILE * TILE
    return pl.CostEstimate(
        flops=4 * pairs * HD, bytes_accessed=heads * 8 * ROWS * HD, transcendentals=pairs
    )


def in_vmem():
    return pl.BlockSpec(memory_space=pltpu.VMEM)


def remote_part(first, heads, q, k, v, even, odd):
    return pl.pallas_call(
        functools.partial(remote_kernel, first, heads),
        in_specs=[in_vmem()] * 5,
        out_specs=in_vmem(),
        out_shape=jax.ShapeDtypeStruct((ROWS + LOG_ROWS, heads * HD), jnp.bfloat16),
        compiler_params=pltpu.CompilerParams(vmem_limit_bytes=VMEM_BYTES),
        cost_estimate=cost(heads),
        name="remote_part",
    )(q, k, v, even, odd)


def local_part(splits, q, k, v, sides):
    heads = sum(splits)
    return pl.pallas_call(
        functools.partial(local_kernel, splits),
        in_specs=[in_vmem()] * (3 + len(sides)),
        out_specs=[in_vmem()] * 2,
        out_shape=[
            jax.ShapeDtypeStruct((ROWS, heads * HD), jnp.float32),
            jax.ShapeDtypeStruct((len(splits), HD, HD), jnp.float32),
        ],
        compiler_params=pltpu.CompilerParams(vmem_limit_bytes=VMEM_BYTES),
        cost_estimate=cost(heads),
        name="local_part",
    )(q, k, v, *sides)


def combine_part(chunk, heads, own, logs, theirs, prior):
    groups = len(theirs)
    block = pl.BlockSpec((ROWS, heads * HD), lambda i: (0, chunk))
    specs = [block, pl.BlockSpec((1, HD, HD), lambda i: (chunk, 0, 0))]
    specs += [pl.BlockSpec(t.shape, lambda i: (0, 0)) for t in theirs]
    operands = [own, logs, *theirs]
    aliases = {}
    if prior is not None:
        specs.append(pl.BlockSpec(memory_space=pl.ANY))
        aliases = {len(operands): 0}
        operands.append(prior)
    return pl.pallas_call(
        functools.partial(combine_kernel, chunk, heads, groups),
        grid=(1,),
        in_specs=specs,
        out_specs=block,
        out_shape=jax.ShapeDtypeStruct(own.shape, jnp.bfloat16),
        input_output_aliases=aliases,
        compiler_params=pltpu.CompilerParams(vmem_limit_bytes=VMEM_BYTES),
        cost_estimate=pl.CostEstimate(
            flops=8 * heads * ROWS * HD, bytes_accessed=heads * 8 * ROWS * HD, transcendentals=0
        ),
        name="combine_part",
    )(*operands)


def frame_pairs(first, frames, cores):
    partner = {}
    for i in range(first, frames - 1, 2):
        partner[i], partner[i + 1] = i + 1, i
    return [
        (i * cores + c, partner[i] * cores + c if i in partner else i * cores + cores - 1 - c)
        for i in range(frames)
        for c in range(cores)
    ]


def per_device(query, keys, values):
    features = query.shape[3]
    heads = features // HD
    splits = CHUNKS
    assert sum(splits) == heads
    q = query.reshape(ROWS, features)
    k = keys.reshape(ROWS, features)
    v = values.reshape(ROWS, features)
    frames = lax.axis_size("frame")
    rows = lax.axis_size("row")
    pairs = [frame_pairs(first, frames, lax.axis_size("head")) for first in (0, 1)]
    place = lax.axis_index("frame")
    if rows == 2:
        routes = [([(0, 1), (1, 0)], [(0, 1), (1, 0)])]
    else:
        down = [(i, i + 1) for i in range(rows - 1)]
        up = [(i + 1, i) for i in range(rows - 1)]
        routes = [(down, up), (up, down)]

    bounds, start = [], 0
    for count in splits:
        bounds.append((start, start + count))
        start += count

    got_q, sides = [], []
    q_now, gate = q, ()
    for a, b in bounds:
        a, b = a * HD, b * HD
        sent = q_now[:, a:b]
        got_q.append([lax.ppermute(sent, "row", there) for there, _ in routes])
        k_now, v_now, _ = lax.optimization_barrier((k, v, (sent, gate)))
        gate = got_q[-1]
        halves = []
        for first in (0, 1):
            row = jnp.where(lax.rem(place, 2) == first, TILE, 0)
            half = [lax.dynamic_slice(x, (row, a), (TILE, b - a)) for x in (k_now, v_now)]
            halves.append(jnp.concatenate(half, 0))
        q_now, _ = lax.optimization_barrier((q, halves))
        sides.append([lax.ppermute(h, ("frame", "head"), p) for h, p in zip(halves, pairs)])

    answers = []
    k_now, v_now = k, v
    for (a, b), chunk_q, (even, odd) in zip(bounds, got_q, sides):
        parts = [remote_part(a, b - a, one, k_now, v_now, even, odd) for one in chunk_q]
        answers.append(parts)
        k_now, v_now, _ = lax.optimization_barrier((k, v, parts))

    q_local, _ = lax.optimization_barrier((q, answers))
    own, logs = local_part(splits, q_local, k, v, [s for pair in sides for s in pair])

    out = None
    for c, ((a, b), parts) in enumerate(zip(bounds, answers)):
        theirs = [lax.ppermute(p, "row", back) for p, (_, back) in zip(parts, routes)]
        out = combine_part(c, b - a, own, logs, theirs, out)
    return out.reshape(query.shape)


def solution(mesh):
    spec = P(("clips", "frame"), "row", None, "head")
    return jax.shard_map(
        per_device, mesh=mesh, in_specs=(spec,) * 3, out_specs=spec, check_vma=False
    )
```

```python
import functools
import math

import jax
import jax.numpy as jnp
from jax import lax
from jax.experimental import pallas as pl
from jax.experimental.pallas import tpu as pltpu
from jax.sharding import PartitionSpec as P

HD = 128
TF = 4
TR = 8
TC = 8
TILE = TF * TR * TC
ROWS = 2 * TILE
EXPONENT = math.log2(math.e) / math.sqrt(HD)
NT = (((1,), (1,)), ((), ()))
NN = (((1,), (0,)), ((), ()))
BLOCKS = ROWS // HD
LOG_ROWS = 16
CHUNKS = (3, 3)
TAILS = (0, 1)
VMEM_BYTES = 48 * 1024 * 1024


def dot(a, b, dims):
    return lax.dot_general(a, b, dims, preferred_element_type=jnp.float32)


def attend(first, heads, q, k, v, even, odd, store):
    place = lax.axis_index("frame")
    present = (place > 0, place < lax.axis_size("frame") - 1)
    is_even = lax.rem(place, 2) == 0
    ones = jnp.ones((ROWS, HD), jnp.bfloat16)
    lanes = lax.broadcasted_iota(jnp.int32, (HD, HD), 1)
    logs = jnp.zeros((HD, HD), jnp.float32)
    for t in range(2):
        rows = slice(t * TILE, (t + 1) * TILE)
        near, far = (odd, even) if t == 0 else (even, odd)
        for j in range(heads):
            here = slice(j * HD, (j + 1) * HD)
            own = slice((first + j) * HD, (first + j + 1) * HD)
            q_tile = q[rows, here]
            k_own = k[:, own]
            v_own = jnp.concatenate([v[:, own], ones], 1)
            side = jnp.where(is_even, near[:, here], far[:, here])
            k_side = jnp.where(present[t], side[:TILE], k_own[:TILE])
            v_side = jnp.concatenate([side[TILE:], ones[:TILE]], 1)
            v_side = jnp.where(present[t], v_side, jnp.zeros_like(v_side))
            s_own = dot(q_tile, k_own, NT)
            s_side = dot(q_tile, k_side, NT)
            peak = jnp.maximum(
                jnp.max(s_own, axis=1, keepdims=True), jnp.max(s_side, axis=1, keepdims=True)
            )
            w_own = jnp.exp2((s_own - peak) * EXPONENT).astype(jnp.bfloat16)
            w_side = jnp.exp2((s_side - peak) * EXPONENT).astype(jnp.bfloat16)
            summed = dot(w_own, v_own, NN) + dot(w_side, v_side, NN)
            total = summed[:, HD:]
            store(rows, here, summed[:, :HD] / total)
            log = peak * EXPONENT + jnp.log2(total[:, :1])
            for i in range(TILE // HD):
                at = (t * (TILE // HD) + i) * (LOG_ROWS // BLOCKS) + j
                logs = jnp.where(lanes == at, log[i * HD : (i + 1) * HD], logs)
    return logs


def pack_logs(logs):
    flat = logs.T[:LOG_ROWS]
    high = flat.astype(jnp.bfloat16)
    return jnp.concatenate([high, (flat - high.astype(jnp.float32)).astype(jnp.bfloat16)], 1)


def unpack_logs(packed):
    parts = packed.astype(jnp.float32)
    flat = parts[:, :HD] + parts[:, HD:]
    return jnp.concatenate([flat, jnp.zeros((HD - LOG_ROWS, HD), jnp.float32)], 0).T


def remote_kernel(first, heads, tail, q, k, v, even, odd, out, *last):
    def store(rows, here, block):
        start = here.start - (heads - tail) * HD
        if start < 0:
            out[rows, here] = block.astype(out.dtype)
        else:
            last[0][rows, start : start + HD] = block.astype(out.dtype)

    packed = pack_logs(attend(first, heads, q, k, v, even, odd, store))
    out[ROWS:, : 2 * HD] = packed
    if out.shape[1] > 2 * HD:
        out[ROWS:, 2 * HD :] = jnp.zeros((LOG_ROWS, out.shape[1] - 2 * HD), out.dtype)


def local_kernel(splits, q, k, v, *rest):
    sides, out, logs = rest[: -1 - len(splits)], rest[-1 - len(splits)], rest[-len(splits) :]
    first = 0
    for c, heads in enumerate(splits):
        columns = slice(first * HD, (first + heads) * HD)

        def store(rows, here, block, first=first):
            out[rows, first * HD + here.start : first * HD + here.stop] = block

        logs[c][...] = attend(
            first, heads, q.at[:, columns], k, v, sides[2 * c], sides[2 * c + 1], store
        )
        first += heads


def shares_of(logs, theirs):
    place = lax.axis_index("row")
    if len(theirs) == 1:
        there = (None,)
    else:
        there = (place < lax.axis_size("row") - 1, place > 0)
    all_logs = [logs[...]]
    for valid, part in zip(there, theirs):
        got = unpack_logs(part[ROWS:, : 2 * HD])
        all_logs.append(got if valid is None else jnp.where(valid, got, -jnp.inf))
    top = functools.reduce(jnp.maximum, all_logs)
    weights = [jnp.exp2(x - top) for x in all_logs]
    total = functools.reduce(jnp.add, weights)
    return [w / total for w in weights]


def write_columns(first, heads, mixed, out, done, fill):
    copies = []
    for b in range(BLOCKS):
        rows = slice(b * HD, (b + 1) * HD)
        fill(b, rows)
        copies.append(
            pltpu.make_async_copy(
                mixed.at[rows, :],
                out.at[rows, first * HD : (first + heads) * HD],
                done.at[b],
            )
        )
        copies[-1].start()
    return copies


def merge_kernel(first, heads, tail, groups, own, logs, *rest):
    theirs, (mixed, done) = rest[:groups], rest[-2:]
    out, *later = rest[-3 - (1 + groups) * (tail > 0) : -2]
    shares = shares_of(logs, theirs)

    def fill(b, rows):
        for j in range(heads):
            here = slice(j * HD, (j + 1) * HD)
            at = b * (LOG_ROWS // BLOCKS) + j
            summed = shares[0][:, at : at + 1] * own[rows, (first + j) * HD : (first + j + 1) * HD]
            for share, part in zip(shares[1:], theirs):
                summed = summed + share[:, at : at + 1] * part[rows, here].astype(jnp.float32)
            mixed[rows, here] = summed.astype(mixed.dtype)

    copies = write_columns(first, heads, mixed, out, done, fill)
    for b in range(BLOCKS):
        for j in range(tail):
            rows, here = slice(b * HD, (b + 1) * HD), slice(j * HD, (j + 1) * HD)
            at = b * (LOG_ROWS // BLOCKS) + heads + j
            own_at = (first + heads + j) * HD
            later[0][rows, here] = shares[0][:, at : at + 1] * own[rows, own_at : own_at + HD]
            for share, spread in zip(shares[1:], later[1:]):
                spread[rows, here] = jnp.broadcast_to(share[:, at : at + 1], (HD, HD))
    for copy in copies:
        copy.wait()


def finish_kernel(first, heads, groups, scaled, *rest):
    shares, theirs = rest[:groups], rest[groups : 2 * groups]
    out, mixed, done = rest[-3:]

    def fill(b, rows):
        summed = scaled[rows, :]
        for share, part in zip(shares, theirs):
            summed = summed + share[rows, :] * part[rows, :].astype(jnp.float32)
        mixed[rows, :] = summed.astype(mixed.dtype)

    for copy in write_columns(first, heads, mixed, out, done, fill):
        copy.wait()


def cost(heads, tiles=6):
    pairs = heads * tiles * TILE * TILE
    return pl.CostEstimate(
        flops=4 * pairs * HD, bytes_accessed=heads * 8 * ROWS * HD, transcendentals=pairs
    )


def in_vmem():
    return pl.BlockSpec(memory_space=pltpu.VMEM)


def remote_part(first, heads, tail, q, k, v, even, odd):
    shapes = [(ROWS + LOG_ROWS, (heads - tail) * HD)] + [(ROWS, tail * HD)] * (tail > 0)
    return pl.pallas_call(
        functools.partial(remote_kernel, first, heads, tail),
        in_specs=[in_vmem()] * 5,
        out_specs=[in_vmem()] * len(shapes),
        out_shape=[jax.ShapeDtypeStruct(shape, jnp.bfloat16) for shape in shapes],
        compiler_params=pltpu.CompilerParams(vmem_limit_bytes=VMEM_BYTES),
        cost_estimate=cost(heads),
        name="remote_part",
    )(q, k, v, even, odd)


def local_part(splits, q, k, v, sides):
    heads = sum(splits)
    return pl.pallas_call(
        functools.partial(local_kernel, splits),
        in_specs=[in_vmem()] * (3 + len(sides)),
        out_specs=[in_vmem()] * (1 + len(splits)),
        out_shape=[
            jax.ShapeDtypeStruct((ROWS, heads * HD), jnp.float32),
            *[jax.ShapeDtypeStruct((HD, HD), jnp.float32) for _ in splits],
        ],
        compiler_params=pltpu.CompilerParams(vmem_limit_bytes=VMEM_BYTES),
        cost_estimate=cost(heads),
        name="local_part",
    )(q, k, v, *sides)


def merge_cost(heads):
    return pl.CostEstimate(
        flops=4 * heads * ROWS * HD, bytes_accessed=heads * 8 * ROWS * HD, transcendentals=0
    )


def copy_scratch(heads):
    return [pltpu.VMEM((ROWS, heads * HD), jnp.bfloat16), pltpu.SemaphoreType.DMA((BLOCKS,))]


def merge_part(first, heads, tail, own, logs, theirs, prior):
    groups = len(theirs)
    later = [jax.ShapeDtypeStruct((ROWS, tail * HD), jnp.float32)] * ((1 + groups) * (tail > 0))
    out, *later = pl.pallas_call(
        functools.partial(merge_kernel, first, heads, tail, groups),
        in_specs=[in_vmem()] * (2 + groups) + [pl.BlockSpec(memory_space=pl.ANY)] * len(prior),
        out_specs=[pl.BlockSpec(memory_space=pl.ANY)] + [in_vmem()] * len(later),
        out_shape=[jax.ShapeDtypeStruct(own.shape, jnp.bfloat16)] + later,
        scratch_shapes=copy_scratch(heads),
        input_output_aliases={2 + groups: 0} if prior else {},
        compiler_params=pltpu.CompilerParams(vmem_limit_bytes=VMEM_BYTES),
        cost_estimate=merge_cost(heads + tail),
        name="merge_part",
    )(own, logs, *theirs, *prior)
    return out, later


def finish_part(first, heads, scaled, shares, theirs, out):
    groups = len(theirs)
    return pl.pallas_call(
        functools.partial(finish_kernel, first, heads, groups),
        in_specs=[in_vmem()] * (1 + 2 * groups) + [pl.BlockSpec(memory_space=pl.ANY)],
        out_specs=pl.BlockSpec(memory_space=pl.ANY),
        out_shape=jax.ShapeDtypeStruct(out.shape, out.dtype),
        scratch_shapes=copy_scratch(heads),
        input_output_aliases={1 + 2 * groups: 0},
        compiler_params=pltpu.CompilerParams(vmem_limit_bytes=VMEM_BYTES),
        cost_estimate=merge_cost(heads),
        name="finish_part",
    )(scaled, *shares, *theirs, out)


def frame_pairs(first, frames, cores):
    partner = {}
    for i in range(first, frames - 1, 2):
        partner[i], partner[i + 1] = i + 1, i
    return [
        (i * cores + c, partner[i] * cores + c if i in partner else i * cores + cores - 1 - c)
        for i in range(frames)
        for c in range(cores)
    ]


def per_device(query, keys, values):
    features = query.shape[3]
    heads = features // HD
    splits = CHUNKS
    assert sum(splits) == heads
    q = query.reshape(ROWS, features)
    k = keys.reshape(ROWS, features)
    v = values.reshape(ROWS, features)
    frames = lax.axis_size("frame")
    rows = lax.axis_size("row")
    pairs = [frame_pairs(first, frames, lax.axis_size("head")) for first in (0, 1)]
    place = lax.axis_index("frame")
    if rows == 2:
        routes = [([(0, 1), (1, 0)], [(0, 1), (1, 0)])]
    else:
        down = [(i, i + 1) for i in range(rows - 1)]
        up = [(i + 1, i) for i in range(rows - 1)]
        routes = [(down, up), (up, down)]

    bounds, start = [], 0
    for count in splits:
        bounds.append((start, start + count))
        start += count

    got_q, sides = [], []
    q_now, gate = q, ()
    for a, b in bounds:
        a, b = a * HD, b * HD
        sent = q_now[:, a:b]
        got_q.append([lax.ppermute(sent, "row", there) for there, _ in routes])
        k_now, v_now, _ = lax.optimization_barrier((k, v, (sent, gate)))
        gate = got_q[-1]
        halves = []
        for first in (0, 1):
            row = jnp.where(lax.rem(place, 2) == first, TILE, 0)
            half = [lax.dynamic_slice(x, (row, a), (TILE, b - a)) for x in (k_now, v_now)]
            halves.append(jnp.concatenate(half, 0))
        q_now, _ = lax.optimization_barrier((q, halves))
        sides.append([lax.ppermute(h, ("frame", "head"), p) for h, p in zip(halves, pairs)])

    answers = []
    k_now, v_now = k, v
    for (a, b), tail, chunk_q, (even, odd) in zip(bounds, TAILS, got_q, sides):
        parts = [remote_part(a, b - a, tail, one, k_now, v_now, even, odd) for one in chunk_q]
        answers.append([list(x) for x in zip(*parts)])
        k_now, v_now, _ = lax.optimization_barrier((k, v, parts))

    back = [route for _, route in routes]

    def send_back(parts):
        return [lax.ppermute(x, "row", p) for x, p in zip(parts, back)]

    q_local, _ = lax.optimization_barrier((q, answers))
    own, *logs = local_part(splits, q_local, k, v, [s for pair in sides for s in pair])
    out = ()
    for (a, b), tail, log, parts in zip(bounds, TAILS, logs, answers):
        theirs = send_back(parts[0])
        out, later = merge_part(a, b - a - tail, tail, own, log, theirs, out)
        if tail:
            last, _ = lax.optimization_barrier((parts[1], log))
            out = finish_part(b - tail, tail, later[0], later[1:], send_back(last), out)
        out = (out,)
    (out,) = out
    return out.reshape(query.shape)


def solution(mesh):
    spec = P(("clips", "frame"), "row", None, "head")
    return jax.shard_map(
        per_device, mesh=mesh, in_specs=(spec,) * 3, out_specs=spec, check_vma=False
    )
```

```python
import functools
import math

import jax
import jax.numpy as jnp
from jax import lax
from jax.experimental import pallas as pl
from jax.experimental.pallas import tpu as pltpu
from jax.sharding import PartitionSpec as P

HD = 128
TF = 4
TR = 8
TC = 8
TILE = TF * TR * TC
ROWS = 2 * TILE
EXPONENT = math.log2(math.e) / math.sqrt(HD)
NT = (((1,), (1,)), ((), ()))
NN = (((1,), (0,)), ((), ()))
BLOCKS = ROWS // HD
LOG_ROWS = 16
CHUNKS = (3, 3)
LEADS = (1, 0)
TAILS = (0, 1)
CYCLES = (((2, 0), (0, 1), (1, 3), (3, 2)), ((0, 2), (2, 3), (3, 1), (1, 0)))
VMEM_BYTES = 48 * 1024 * 1024


def dot(a, b, dims):
    return lax.dot_general(a, b, dims, preferred_element_type=jnp.float32)


def attend(first, heads, q, k, v, even, odd, store, slot=0):
    place = lax.axis_index("frame")
    present = (place > 0, place < lax.axis_size("frame") - 1)
    is_even = lax.rem(place, 2) == 0
    ones = jnp.ones((ROWS, HD), jnp.bfloat16)
    lanes = lax.broadcasted_iota(jnp.int32, (HD, HD), 1)
    logs = jnp.zeros((HD, HD), jnp.float32)
    for t in range(2):
        rows = slice(t * TILE, (t + 1) * TILE)
        near, far = (odd, even) if t == 0 else (even, odd)
        for j in range(heads):
            here = slice(j * HD, (j + 1) * HD)
            own = slice((first + j) * HD, (first + j + 1) * HD)
            q_tile = q[rows, here]
            k_own = k[:, own]
            v_own = jnp.concatenate([v[:, own], ones], 1)
            side = jnp.where(is_even, near[:, here], far[:, here])
            k_side = jnp.where(present[t], side[:TILE], k_own[:TILE])
            v_side = jnp.concatenate([side[TILE:], ones[:TILE]], 1)
            v_side = jnp.where(present[t], v_side, jnp.zeros_like(v_side))
            s_own = dot(q_tile, k_own, NT)
            s_side = dot(q_tile, k_side, NT)
            peak = jnp.maximum(
                jnp.max(s_own, axis=1, keepdims=True), jnp.max(s_side, axis=1, keepdims=True)
            )
            w_own = jnp.exp2((s_own - peak) * EXPONENT).astype(jnp.bfloat16)
            w_side = jnp.exp2((s_side - peak) * EXPONENT).astype(jnp.bfloat16)
            summed = dot(w_own, v_own, NN) + dot(w_side, v_side, NN)
            total = summed[:, HD:]
            store(rows, here, summed[:, :HD] / total)
            log = peak * EXPONENT + jnp.log2(total[:, :1])
            for i in range(TILE // HD):
                at = (t * (TILE // HD) + i) * (LOG_ROWS // BLOCKS) + slot + j
                logs = jnp.where(lanes == at, log[i * HD : (i + 1) * HD], logs)
    return logs


def pack_logs(logs):
    flat = logs.T[:LOG_ROWS]
    high = flat.astype(jnp.bfloat16)
    return jnp.concatenate([high, (flat - high.astype(jnp.float32)).astype(jnp.bfloat16)], 1)


def unpack_logs(packed):
    parts = packed.astype(jnp.float32)
    flat = parts[:, :HD] + parts[:, HD:]
    return jnp.concatenate([flat, jnp.zeros((HD - LOG_ROWS, HD), jnp.float32)], 0).T


def lead_kernel(first, heads, q, k, v, even, odd, out, logs):
    def store(rows, here, block):
        out[rows, here] = block.astype(out.dtype)

    logs[...] = attend(first, heads, q, k, v, even, odd, store)


def remote_kernel(first, heads, lead, tail, q, k, v, even, odd, *rest):
    earlier, (out, *last) = rest[: lead > 0], rest[lead > 0 :]

    def store(rows, here, block):
        start = here.start - (heads - tail) * HD
        if start < 0:
            out[rows, here] = block.astype(out.dtype)
        else:
            last[0][rows, start : start + HD] = block.astype(out.dtype)

    q_here = q.at[:, lead * HD : (lead + heads) * HD]
    sides = [x.at[:, lead * HD : (lead + heads) * HD] for x in (even, odd)]
    logs = attend(first, heads, q_here, k, v, *sides, store, lead)
    packed = pack_logs(logs + earlier[0][...] if lead else logs)
    out[ROWS:, : 2 * HD] = packed
    if out.shape[1] > 2 * HD:
        out[ROWS:, 2 * HD :] = jnp.zeros((LOG_ROWS, out.shape[1] - 2 * HD), out.dtype)


def local_kernel(splits, q, k, v, *rest):
    sides, out, logs = rest[: -1 - len(splits)], rest[-1 - len(splits)], rest[-len(splits) :]
    first = 0
    for c, heads in enumerate(splits):
        columns = slice(first * HD, (first + heads) * HD)

        def store(rows, here, block, first=first):
            out[rows, first * HD + here.start : first * HD + here.stop] = block

        logs[c][...] = attend(
            first, heads, q.at[:, columns], k, v, sides[2 * c], sides[2 * c + 1], store
        )
        first += heads


def shares_of(logs, theirs):
    place = lax.axis_index("row")
    if len(theirs) == 1:
        there = (None,)
    else:
        there = (place < lax.axis_size("row") - 1, place > 0)
    all_logs = [logs[...]]
    for valid, part in zip(there, theirs):
        got = unpack_logs(part[ROWS:, : 2 * HD])
        all_logs.append(got if valid is None else jnp.where(valid, got, -jnp.inf))
    top = functools.reduce(jnp.maximum, all_logs)
    weights = [jnp.exp2(x - top) for x in all_logs]
    total = functools.reduce(jnp.add, weights)
    return [w / total for w in weights]


def write_columns(first, heads, mixed, out, done, fill):
    copies = []
    for b in range(BLOCKS):
        rows = slice(b * HD, (b + 1) * HD)
        fill(b, rows)
        copies.append(
            pltpu.make_async_copy(
                mixed.at[rows, :],
                out.at[rows, first * HD : (first + heads) * HD],
                done.at[b],
            )
        )
        copies[-1].start()
    return copies


def merge_kernel(first, lead, heads, tail, groups, own, logs, *rest):
    leads, rest = rest[: groups * (lead > 0)], rest[groups * (lead > 0) :]
    theirs, (mixed, done) = rest[:groups], rest[-2:]
    out, *later = rest[-3 - (1 + groups) * (tail > 0) : -2]
    shares = shares_of(logs, theirs)

    def fill(b, rows):
        for j in range(heads):
            here = slice(j * HD, (j + 1) * HD)
            at = b * (LOG_ROWS // BLOCKS) + j
            summed = shares[0][:, at : at + 1] * own[rows, (first + j) * HD : (first + j + 1) * HD]
            parts, start = (leads, j * HD) if j < lead else (theirs, (j - lead) * HD)
            for share, part in zip(shares[1:], parts):
                block = part[rows, start : start + HD].astype(jnp.float32)
                summed = summed + share[:, at : at + 1] * block
            mixed[rows, here] = summed.astype(mixed.dtype)

    copies = write_columns(first, heads, mixed, out, done, fill)
    for b in range(BLOCKS):
        for j in range(tail):
            rows, here = slice(b * HD, (b + 1) * HD), slice(j * HD, (j + 1) * HD)
            at = b * (LOG_ROWS // BLOCKS) + heads + j
            own_at = (first + heads + j) * HD
            later[0][rows, here] = shares[0][:, at : at + 1] * own[rows, own_at : own_at + HD]
            for share, spread in zip(shares[1:], later[1:]):
                spread[rows, here] = jnp.broadcast_to(share[:, at : at + 1], (HD, HD))
    for copy in copies:
        copy.wait()


def finish_kernel(first, heads, groups, turn, scaled, *rest):
    shares, theirs = rest[:groups], rest[groups : 2 * groups]
    out, mixed, done = rest[-3:]

    def fill(b, rows):
        summed = scaled[rows, :]
        for share, part in zip(shares, theirs):
            summed = summed + share[rows, :] * part[rows, :].astype(jnp.float32)
        mixed[rows, :] = summed.astype(mixed.dtype)

    def finish():
        for copy in write_columns(first, heads, mixed, out, done, fill):
            copy.wait()

    if turn is None:
        finish()
    else:
        place = lax.axis_index("row") + lax.axis_index("head")
        pl.when(lax.rem(place, 2) == turn)(finish)


def cost(heads, tiles=6):
    pairs = heads * tiles * TILE * TILE
    return pl.CostEstimate(
        flops=4 * pairs * HD, bytes_accessed=heads * 8 * ROWS * HD, transcendentals=pairs
    )


def in_vmem():
    return pl.BlockSpec(memory_space=pltpu.VMEM)


def lead_part(first, heads, q, k, v, even, odd):
    return pl.pallas_call(
        functools.partial(lead_kernel, first, heads),
        in_specs=[in_vmem()] * 5,
        out_specs=[in_vmem()] * 2,
        out_shape=[
            jax.ShapeDtypeStruct((ROWS, heads * HD), jnp.bfloat16),
            jax.ShapeDtypeStruct((HD, HD), jnp.float32),
        ],
        compiler_params=pltpu.CompilerParams(vmem_limit_bytes=VMEM_BYTES),
        cost_estimate=cost(heads),
        name="lead_part",
    )(q, k, v, even, odd)


def remote_part(first, heads, lead, tail, q, k, v, even, odd, *earlier):
    shapes = [(ROWS + LOG_ROWS, (heads - tail) * HD)] + [(ROWS, tail * HD)] * (tail > 0)
    return pl.pallas_call(
        functools.partial(remote_kernel, first, heads, lead, tail),
        in_specs=[in_vmem()] * (5 + len(earlier)),
        out_specs=[in_vmem()] * len(shapes),
        out_shape=[jax.ShapeDtypeStruct(shape, jnp.bfloat16) for shape in shapes],
        compiler_params=pltpu.CompilerParams(vmem_limit_bytes=VMEM_BYTES),
        cost_estimate=cost(heads),
        name="remote_part",
    )(q, k, v, even, odd, *earlier)


def local_part(splits, q, k, v, sides):
    heads = sum(splits)
    return pl.pallas_call(
        functools.partial(local_kernel, splits),
        in_specs=[in_vmem()] * (3 + len(sides)),
        out_specs=[in_vmem()] * (1 + len(splits)),
        out_shape=[
            jax.ShapeDtypeStruct((ROWS, heads * HD), jnp.float32),
            *[jax.ShapeDtypeStruct((HD, HD), jnp.float32) for _ in splits],
        ],
        compiler_params=pltpu.CompilerParams(vmem_limit_bytes=VMEM_BYTES),
        cost_estimate=cost(heads),
        name="local_part",
    )(q, k, v, *sides)


def merge_cost(heads):
    return pl.CostEstimate(
        flops=4 * heads * ROWS * HD, bytes_accessed=heads * 8 * ROWS * HD, transcendentals=0
    )


def copy_scratch(heads):
    return [pltpu.VMEM((ROWS, heads * HD), jnp.bfloat16), pltpu.SemaphoreType.DMA((BLOCKS,))]


def merge_part(first, lead, heads, tail, own, logs, leads, theirs, prior):
    groups = len(theirs)
    count = len(leads) + groups
    later = [jax.ShapeDtypeStruct((ROWS, tail * HD), jnp.float32)] * ((1 + groups) * (tail > 0))
    out, *later = pl.pallas_call(
        functools.partial(merge_kernel, first, lead, heads, tail, groups),
        in_specs=[in_vmem()] * (2 + count) + [pl.BlockSpec(memory_space=pl.ANY)] * len(prior),
        out_specs=[pl.BlockSpec(memory_space=pl.ANY)] + [in_vmem()] * len(later),
        out_shape=[jax.ShapeDtypeStruct(own.shape, jnp.bfloat16)] + later,
        scratch_shapes=copy_scratch(heads),
        input_output_aliases={2 + count: 0} if prior else {},
        compiler_params=pltpu.CompilerParams(vmem_limit_bytes=VMEM_BYTES),
        cost_estimate=merge_cost(heads + tail),
        name="merge_part",
    )(own, logs, *leads, *theirs, *prior)
    return out, later


def finish_part(first, heads, scaled, shares, theirs, out, turn=None):
    groups = len(theirs)
    return pl.pallas_call(
        functools.partial(finish_kernel, first, heads, groups, turn),
        in_specs=[in_vmem()] * (1 + 2 * groups) + [pl.BlockSpec(memory_space=pl.ANY)],
        out_specs=pl.BlockSpec(memory_space=pl.ANY),
        out_shape=jax.ShapeDtypeStruct(out.shape, out.dtype),
        scratch_shapes=copy_scratch(heads),
        input_output_aliases={1 + 2 * groups: 0},
        compiler_params=pltpu.CompilerParams(vmem_limit_bytes=VMEM_BYTES),
        cost_estimate=merge_cost(heads),
        name="finish_part",
    )(scaled, *shares, *theirs, out)


def frame_pairs(first, frames, cores):
    partner = {}
    for i in range(first, frames - 1, 2):
        partner[i], partner[i + 1] = i + 1, i
    return [
        (i * cores + c, partner[i] * cores + c if i in partner else i * cores + cores - 1 - c)
        for i in range(frames)
        for c in range(cores)
    ]


def per_device(query, keys, values):
    features = query.shape[3]
    heads = features // HD
    splits = CHUNKS
    assert sum(splits) == heads
    q = query.reshape(ROWS, features)
    k = keys.reshape(ROWS, features)
    v = values.reshape(ROWS, features)
    frames = lax.axis_size("frame")
    rows = lax.axis_size("row")
    pairs = [frame_pairs(first, frames, lax.axis_size("head")) for first in (0, 1)]
    place = lax.axis_index("frame")
    if rows == 2:
        routes = [([(0, 1), (1, 0)], [(0, 1), (1, 0)])]
    else:
        down = [(i, i + 1) for i in range(rows - 1)]
        up = [(i + 1, i) for i in range(rows - 1)]
        routes = [(down, up), (up, down)]

    bounds, start = [], 0
    for count in splits:
        bounds.append((start, start + count))
        start += count

    got_q, sides = [], []
    q_now, gate = q, ()
    for a, b in bounds:
        a, b = a * HD, b * HD
        sent = q_now[:, a:b]
        got_q.append([lax.ppermute(sent, "row", there) for there, _ in routes])
        k_now, v_now, _ = lax.optimization_barrier((k, v, (sent, gate)))
        gate = got_q[-1]
        halves = []
        for first in (0, 1):
            row = jnp.where(lax.rem(place, 2) == first, TILE, 0)
            half = [lax.dynamic_slice(x, (row, a), (TILE, b - a)) for x in (k_now, v_now)]
            halves.append(jnp.concatenate(half, 0))
        q_now, _ = lax.optimization_barrier((q, halves))
        sides.append([lax.ppermute(h, ("frame", "head"), p) for h, p in zip(halves, pairs)])

    back = [route for _, route in routes]

    def send_back(parts):
        return [lax.ppermute(x, "row", p) for x, p in zip(parts, back)]

    answers, led = [], []
    k_now, v_now = k, v
    for (a, b), lead, tail, chunk_q, (even, odd) in zip(bounds, LEADS, TAILS, got_q, sides):
        parts, firsts = [], []
        for one in chunk_q:
            operands, earlier = (one, k_now, v_now, even, odd), ()
            if lead:
                block, *earlier = lead_part(a, lead, *operands)
                firsts.append(block)
                k_now, v_now, _ = lax.optimization_barrier((k, v, block))
                operands = (one, k_now, v_now, even, odd)
            parts.append(remote_part(a + lead, b - a - lead, lead, tail, *operands, *earlier))
        led.append(send_back(firsts))
        answers.append([list(x) for x in zip(*parts)])
        k_now, v_now, _ = lax.optimization_barrier((k, v, (parts, led[-1])))

    q_local, _ = lax.optimization_barrier((q, answers))
    own, *logs = local_part(splits, q_local, k, v, [s for pair in sides for s in pair])
    out = ()
    for (a, b), lead, tail, log, leads, parts in zip(bounds, LEADS, TAILS, logs, led, answers):
        theirs = send_back(parts[0])
        out, later = merge_part(a, lead, b - a - tail, tail, own, log, leads, theirs, out)
        if tail:
            last, _ = lax.optimization_barrier((parts[1], log))
            if rows == 2 and lax.axis_size("head") == 2:
                for turn, cycle in enumerate(CYCLES):
                    came = [lax.ppermute(last[0], ("row", "head"), cycle)]
                    out = finish_part(b - tail, tail, later[0], later[1:], came, out, turn)
            else:
                out = finish_part(b - tail, tail, later[0], later[1:], send_back(last), out)
        out = (out,)
    (out,) = out
    return out.reshape(query.shape)


def solution(mesh):
    spec = P(("clips", "frame"), "row", None, "head")
    return jax.shard_map(
        per_device, mesh=mesh, in_specs=(spec,) * 3, out_specs=spec, check_vma=False
    )
```

```python
import functools
import math

import jax
import jax.numpy as jnp
from jax import lax
from jax.experimental import pallas as pl
from jax.experimental.pallas import tpu as pltpu
from jax.sharding import PartitionSpec as P

HD = 128
TF = 4
TR = 8
TC = 8
TILE = TF * TR * TC
ROWS = 2 * TILE
EXPONENT = math.log2(math.e) / math.sqrt(HD)
NT = (((1,), (1,)), ((), ()))
NN = (((1,), (0,)), ((), ()))
BLOCKS = ROWS // HD
LOG_ROWS = 16
CHUNKS = (3, 3)
LEADS = (1, 0)
TAILS = (0, 1)
CYCLES = (((0, 2), (2, 3), (3, 1), (1, 0)), ((2, 0), (0, 1), (1, 3), (3, 2)))
VMEM_BYTES = 48 * 1024 * 1024


def dot(a, b, dims):
    return lax.dot_general(a, b, dims, preferred_element_type=jnp.float32)


def attend(first, heads, q, k, v, even, odd, store, slot=0):
    place = lax.axis_index("frame")
    present = (place > 0, place < lax.axis_size("frame") - 1)
    is_even = lax.rem(place, 2) == 0
    ones = jnp.ones((ROWS, HD), jnp.bfloat16)
    lanes = lax.broadcasted_iota(jnp.int32, (HD, HD), 1)
    logs = jnp.zeros((HD, HD), jnp.float32)
    for t in range(2):
        rows = slice(t * TILE, (t + 1) * TILE)
        near, far = (odd, even) if t == 0 else (even, odd)
        for j in range(heads):
            here = slice(j * HD, (j + 1) * HD)
            own = slice((first + j) * HD, (first + j + 1) * HD)
            q_tile = q[rows, here]
            k_own = k[:, own]
            v_own = jnp.concatenate([v[:, own], ones], 1)
            side = jnp.where(is_even, near[:, here], far[:, here])
            k_side = jnp.where(present[t], side[:TILE], k_own[:TILE])
            v_side = jnp.concatenate([side[TILE:], ones[:TILE]], 1)
            v_side = jnp.where(present[t], v_side, jnp.zeros_like(v_side))
            s_own = dot(q_tile, k_own, NT)
            s_side = dot(q_tile, k_side, NT)
            peak = jnp.maximum(
                jnp.max(s_own, axis=1, keepdims=True), jnp.max(s_side, axis=1, keepdims=True)
            )
            w_own = jnp.exp2((s_own - peak) * EXPONENT).astype(jnp.bfloat16)
            w_side = jnp.exp2((s_side - peak) * EXPONENT).astype(jnp.bfloat16)
            summed = dot(w_own, v_own, NN) + dot(w_side, v_side, NN)
            total = summed[:, HD:]
            store(rows, here, summed[:, :HD] / total)
            log = peak * EXPONENT + jnp.log2(total[:, :1])
            for i in range(TILE // HD):
                at = (t * (TILE // HD) + i) * (LOG_ROWS // BLOCKS) + slot + j
                logs = jnp.where(lanes == at, log[i * HD : (i + 1) * HD], logs)
    return logs


def pack_logs(logs):
    flat = logs.T[:LOG_ROWS]
    high = flat.astype(jnp.bfloat16)
    return jnp.concatenate([high, (flat - high.astype(jnp.float32)).astype(jnp.bfloat16)], 1)


def unpack_logs(packed):
    parts = packed.astype(jnp.float32)
    flat = parts[:, :HD] + parts[:, HD:]
    return jnp.concatenate([flat, jnp.zeros((HD - LOG_ROWS, HD), jnp.float32)], 0).T


def lead_kernel(first, heads, q, k, v, even, odd, out, logs):
    def store(rows, here, block):
        out[rows, here] = block.astype(out.dtype)

    logs[...] = attend(first, heads, q, k, v, even, odd, store)


def remote_kernel(first, heads, lead, tail, q, k, v, even, odd, *rest):
    earlier, (out, *last) = rest[: lead > 0], rest[lead > 0 :]

    def store(rows, here, block):
        start = here.start - (heads - tail) * HD
        if start < 0:
            out[rows, here] = block.astype(out.dtype)
        else:
            last[0][rows, start : start + HD] = block.astype(out.dtype)

    q_here = q.at[:, lead * HD : (lead + heads) * HD]
    sides = [x.at[:, lead * HD : (lead + heads) * HD] for x in (even, odd)]
    logs = attend(first, heads, q_here, k, v, *sides, store, lead)
    packed = pack_logs(logs + earlier[0][...] if lead else logs)
    out[ROWS:, : 2 * HD] = packed
    if out.shape[1] > 2 * HD:
        out[ROWS:, 2 * HD :] = jnp.zeros((LOG_ROWS, out.shape[1] - 2 * HD), out.dtype)


def local_kernel(splits, q, k, v, *rest):
    sides, out, logs = rest[: -1 - len(splits)], rest[-1 - len(splits)], rest[-len(splits) :]
    first = 0
    for c, heads in enumerate(splits):
        columns = slice(first * HD, (first + heads) * HD)

        def store(rows, here, block, first=first):
            out[rows, first * HD + here.start : first * HD + here.stop] = block

        logs[c][...] = attend(
            first, heads, q.at[:, columns], k, v, sides[2 * c], sides[2 * c + 1], store
        )
        first += heads


def shares_of(logs, theirs):
    place = lax.axis_index("row")
    if len(theirs) == 1:
        there = (None,)
    else:
        there = (place < lax.axis_size("row") - 1, place > 0)
    all_logs = [logs[...]]
    for valid, part in zip(there, theirs):
        got = unpack_logs(part[ROWS:, : 2 * HD])
        all_logs.append(got if valid is None else jnp.where(valid, got, -jnp.inf))
    top = functools.reduce(jnp.maximum, all_logs)
    weights = [jnp.exp2(x - top) for x in all_logs]
    total = functools.reduce(jnp.add, weights)
    return [w / total for w in weights]


def write_columns(first, heads, mixed, out, done, fill):
    copies = []
    for b in range(BLOCKS):
        rows = slice(b * HD, (b + 1) * HD)
        fill(b, rows)
        copies.append(
            pltpu.make_async_copy(
                mixed.at[rows, :],
                out.at[rows, first * HD : (first + heads) * HD],
                done.at[b],
            )
        )
        copies[-1].start()
    return copies


def merge_kernel(first, lead, heads, tail, groups, own, logs, *rest):
    leads, rest = rest[: groups * (lead > 0)], rest[groups * (lead > 0) :]
    theirs, (mixed, done) = rest[:groups], rest[-2:]
    out, *later = rest[-3 - (1 + groups) * (tail > 0) : -2]
    shares = shares_of(logs, theirs)

    def fill(b, rows):
        for j in range(heads):
            here = slice(j * HD, (j + 1) * HD)
            at = b * (LOG_ROWS // BLOCKS) + j
            summed = shares[0][:, at : at + 1] * own[rows, (first + j) * HD : (first + j + 1) * HD]
            parts, start = (leads, j * HD) if j < lead else (theirs, (j - lead) * HD)
            for share, part in zip(shares[1:], parts):
                block = part[rows, start : start + HD].astype(jnp.float32)
                summed = summed + share[:, at : at + 1] * block
            mixed[rows, here] = summed.astype(mixed.dtype)

    copies = write_columns(first, heads, mixed, out, done, fill)
    for b in range(BLOCKS):
        for j in range(tail):
            rows, here = slice(b * HD, (b + 1) * HD), slice(j * HD, (j + 1) * HD)
            at = b * (LOG_ROWS // BLOCKS) + heads + j
            own_at = (first + heads + j) * HD
            later[0][rows, here] = shares[0][:, at : at + 1] * own[rows, own_at : own_at + HD]
            for share, spread in zip(shares[1:], later[1:]):
                spread[rows, here] = jnp.broadcast_to(share[:, at : at + 1], (HD, HD))
    for copy in copies:
        copy.wait()


def finish_kernel(first, heads, groups, turn, scaled, *rest):
    shares, theirs = rest[:groups], rest[groups : 2 * groups]
    out, mixed, done = rest[-3:]

    def fill(b, rows):
        summed = scaled[rows, :]
        for share, part in zip(shares, theirs):
            summed = summed + share[rows, :] * part[rows, :].astype(jnp.float32)
        mixed[rows, :] = summed.astype(mixed.dtype)

    def finish():
        for copy in write_columns(first, heads, mixed, out, done, fill):
            copy.wait()

    if turn is None:
        finish()
    else:
        place = lax.axis_index("row") + lax.axis_index("head")
        pl.when(lax.rem(place, 2) != turn)(finish)


def cost(heads, tiles=6):
    pairs = heads * tiles * TILE * TILE
    return pl.CostEstimate(
        flops=4 * pairs * HD, bytes_accessed=heads * 8 * ROWS * HD, transcendentals=pairs
    )


def in_vmem():
    return pl.BlockSpec(memory_space=pltpu.VMEM)


def lead_part(first, heads, q, k, v, even, odd):
    return pl.pallas_call(
        functools.partial(lead_kernel, first, heads),
        in_specs=[in_vmem()] * 5,
        out_specs=[in_vmem()] * 2,
        out_shape=[
            jax.ShapeDtypeStruct((ROWS, heads * HD), jnp.bfloat16),
            jax.ShapeDtypeStruct((HD, HD), jnp.float32),
        ],
        compiler_params=pltpu.CompilerParams(vmem_limit_bytes=VMEM_BYTES),
        cost_estimate=cost(heads),
        name="lead_part",
    )(q, k, v, even, odd)


def remote_part(first, heads, lead, tail, q, k, v, even, odd, *earlier):
    shapes = [(ROWS + LOG_ROWS, (heads - tail) * HD)] + [(ROWS, tail * HD)] * (tail > 0)
    return pl.pallas_call(
        functools.partial(remote_kernel, first, heads, lead, tail),
        in_specs=[in_vmem()] * (5 + len(earlier)),
        out_specs=[in_vmem()] * len(shapes),
        out_shape=[jax.ShapeDtypeStruct(shape, jnp.bfloat16) for shape in shapes],
        compiler_params=pltpu.CompilerParams(vmem_limit_bytes=VMEM_BYTES),
        cost_estimate=cost(heads),
        name="remote_part",
    )(q, k, v, even, odd, *earlier)


def local_part(splits, q, k, v, sides):
    heads = sum(splits)
    return pl.pallas_call(
        functools.partial(local_kernel, splits),
        in_specs=[in_vmem()] * (3 + len(sides)),
        out_specs=[in_vmem()] * (1 + len(splits)),
        out_shape=[
            jax.ShapeDtypeStruct((ROWS, heads * HD), jnp.float32),
            *[jax.ShapeDtypeStruct((HD, HD), jnp.float32) for _ in splits],
        ],
        compiler_params=pltpu.CompilerParams(vmem_limit_bytes=VMEM_BYTES),
        cost_estimate=cost(heads),
        name="local_part",
    )(q, k, v, *sides)


def merge_cost(heads):
    return pl.CostEstimate(
        flops=4 * heads * ROWS * HD, bytes_accessed=heads * 8 * ROWS * HD, transcendentals=0
    )


def copy_scratch(heads):
    return [pltpu.VMEM((ROWS, heads * HD), jnp.bfloat16), pltpu.SemaphoreType.DMA((BLOCKS,))]


def merge_part(first, lead, heads, tail, own, logs, leads, theirs, prior):
    groups = len(theirs)
    count = len(leads) + groups
    later = [jax.ShapeDtypeStruct((ROWS, tail * HD), jnp.float32)] * ((1 + groups) * (tail > 0))
    out, *later = pl.pallas_call(
        functools.partial(merge_kernel, first, lead, heads, tail, groups),
        in_specs=[in_vmem()] * (2 + count) + [pl.BlockSpec(memory_space=pl.ANY)] * len(prior),
        out_specs=[pl.BlockSpec(memory_space=pl.ANY)] + [in_vmem()] * len(later),
        out_shape=[jax.ShapeDtypeStruct(own.shape, jnp.bfloat16)] + later,
        scratch_shapes=copy_scratch(heads),
        input_output_aliases={2 + count: 0} if prior else {},
        compiler_params=pltpu.CompilerParams(vmem_limit_bytes=VMEM_BYTES),
        cost_estimate=merge_cost(heads + tail),
        name="merge_part",
    )(own, logs, *leads, *theirs, *prior)
    return out, later


def finish_part(first, heads, scaled, shares, theirs, out, turn=None):
    groups = len(theirs)
    return pl.pallas_call(
        functools.partial(finish_kernel, first, heads, groups, turn),
        in_specs=[in_vmem()] * (1 + 2 * groups) + [pl.BlockSpec(memory_space=pl.ANY)],
        out_specs=pl.BlockSpec(memory_space=pl.ANY),
        out_shape=jax.ShapeDtypeStruct(out.shape, out.dtype),
        scratch_shapes=copy_scratch(heads),
        input_output_aliases={1 + 2 * groups: 0},
        compiler_params=pltpu.CompilerParams(vmem_limit_bytes=VMEM_BYTES),
        cost_estimate=merge_cost(heads),
        name="finish_part",
    )(scaled, *shares, *theirs, out)


def frame_pairs(first, frames, cores):
    partner = {}
    for i in range(first, frames - 1, 2):
        partner[i], partner[i + 1] = i + 1, i
    return [
        (i * cores + c, partner[i] * cores + c if i in partner else i * cores + cores - 1 - c)
        for i in range(frames)
        for c in range(cores)
    ]


def per_device(query, keys, values):
    features = query.shape[3]
    heads = features // HD
    splits = CHUNKS
    assert sum(splits) == heads
    q = query.reshape(ROWS, features)
    k = keys.reshape(ROWS, features)
    v = values.reshape(ROWS, features)
    frames = lax.axis_size("frame")
    rows = lax.axis_size("row")
    pairs = [frame_pairs(first, frames, lax.axis_size("head")) for first in (0, 1)]
    place = lax.axis_index("frame")
    if rows == 2:
        routes = [([(0, 1), (1, 0)], [(0, 1), (1, 0)])]
    else:
        down = [(i, i + 1) for i in range(rows - 1)]
        up = [(i + 1, i) for i in range(rows - 1)]
        routes = [(down, up), (up, down)]

    bounds, start = [], 0
    for count in splits:
        bounds.append((start, start + count))
        start += count

    got_q, sides = [], []
    q_now, gate = q, ()
    for a, b in bounds:
        a, b = a * HD, b * HD
        sent = q_now[:, a:b]
        got_q.append([lax.ppermute(sent, "row", there) for there, _ in routes])
        k_now, v_now, _ = lax.optimization_barrier((k, v, (sent, gate)))
        gate = got_q[-1]
        halves = []
        for first in (0, 1):
            row = jnp.where(lax.rem(place, 2) == first, TILE, 0)
            half = [lax.dynamic_slice(x, (row, a), (TILE, b - a)) for x in (k_now, v_now)]
            halves.append(jnp.concatenate(half, 0))
        q_now, _ = lax.optimization_barrier((q, halves))
        sides.append([lax.ppermute(h, ("frame", "head"), p) for h, p in zip(halves, pairs)])

    back = [route for _, route in routes]

    def send_back(parts):
        return [lax.ppermute(x, "row", p) for x, p in zip(parts, back)]

    answers, led = [], []
    k_now, v_now = k, v
    for (a, b), lead, tail, chunk_q, (even, odd) in zip(bounds, LEADS, TAILS, got_q, sides):
        parts, firsts = [], []
        for one in chunk_q:
            operands, earlier = (one, k_now, v_now, even, odd), ()
            if lead:
                block, *earlier = lead_part(a, lead, *operands)
                firsts.append(block)
                k_now, v_now, _ = lax.optimization_barrier((k, v, block))
                operands = (one, k_now, v_now, even, odd)
            parts.append(remote_part(a + lead, b - a - lead, lead, tail, *operands, *earlier))
        led.append(send_back(firsts))
        answers.append([list(x) for x in zip(*parts)])
        k_now, v_now, _ = lax.optimization_barrier((k, v, (parts, led[-1])))

    q_local, _ = lax.optimization_barrier((q, answers))
    own, *logs = local_part(splits, q_local, k, v, [s for pair in sides for s in pair])
    out = ()
    for (a, b), lead, tail, log, leads, parts in zip(bounds, LEADS, TAILS, logs, led, answers):
        theirs = send_back(parts[0])
        out, later = merge_part(a, lead, b - a - tail, tail, own, log, leads, theirs, out)
        if tail:
            last, _ = lax.optimization_barrier((parts[1], log))
            if rows == 2 and lax.axis_size("head") == 2:
                for turn, cycle in enumerate(CYCLES):
                    came = [lax.ppermute(last[0], ("row", "head"), cycle)]
                    out = finish_part(b - tail, tail, later[0], later[1:], came, out, turn)
            else:
                out = finish_part(b - tail, tail, later[0], later[1:], send_back(last), out)
        out = (out,)
    (out,) = out
    return out.reshape(query.shape)


def solution(mesh):
    spec = P(("clips", "frame"), "row", None, "head")
    return jax.shard_map(
        per_device, mesh=mesh, in_specs=(spec,) * 3, out_specs=spec, check_vma=False
    )
```

```python
import functools
import math

import jax
import jax.numpy as jnp
from jax import lax
from jax.experimental import pallas as pl
from jax.experimental.pallas import tpu as pltpu
from jax.sharding import PartitionSpec as P

HD = 128
TF = 4
TR = 8
TC = 8
TILE = TF * TR * TC
ROWS = 2 * TILE
EXPONENT = math.log2(math.e) / math.sqrt(HD)
NT = (((1,), (1,)), ((), ()))
NN = (((1,), (0,)), ((), ()))
BLOCKS = ROWS // HD
LOG_ROWS = 16
CHUNKS = (3, 3)
LEADS = (1, 0)
TAILS = (0, 1)
ONE_ALONG_X = tuple((i, i ^ 2 if i % 2 else i ^ 4) for i in range(8))
ZERO_ALONG_X = tuple((i, i ^ 2) for i in range(0, 8, 2))
VMEM_BYTES = 48 * 1024 * 1024


def dot(a, b, dims):
    return lax.dot_general(a, b, dims, preferred_element_type=jnp.float32)


def attend(first, heads, q, k, v, even, odd, store, slot=0):
    place = lax.axis_index("frame")
    present = (place > 0, place < lax.axis_size("frame") - 1)
    is_even = lax.rem(place, 2) == 0
    ones = jnp.ones((ROWS, HD), jnp.bfloat16)
    lanes = lax.broadcasted_iota(jnp.int32, (HD, HD), 1)
    logs = jnp.zeros((HD, HD), jnp.float32)
    for t in range(2):
        rows = slice(t * TILE, (t + 1) * TILE)
        near, far = (odd, even) if t == 0 else (even, odd)
        for j in range(heads):
            here = slice(j * HD, (j + 1) * HD)
            own = slice((first + j) * HD, (first + j + 1) * HD)
            q_tile = q[rows, here]
            k_own = k[:, own]
            v_own = jnp.concatenate([v[:, own], ones], 1)
            side = jnp.where(is_even, near[:, here], far[:, here])
            k_side = jnp.where(present[t], side[:TILE], k_own[:TILE])
            v_side = jnp.concatenate([side[TILE:], ones[:TILE]], 1)
            v_side = jnp.where(present[t], v_side, jnp.zeros_like(v_side))
            s_own = dot(q_tile, k_own, NT)
            s_side = dot(q_tile, k_side, NT)
            peak = jnp.maximum(
                jnp.max(s_own, axis=1, keepdims=True), jnp.max(s_side, axis=1, keepdims=True)
            )
            w_own = jnp.exp2((s_own - peak) * EXPONENT).astype(jnp.bfloat16)
            w_side = jnp.exp2((s_side - peak) * EXPONENT).astype(jnp.bfloat16)
            summed = dot(w_own, v_own, NN) + dot(w_side, v_side, NN)
            total = summed[:, HD:]
            store(rows, here, summed[:, :HD] / total)
            log = peak * EXPONENT + jnp.log2(total[:, :1])
            for i in range(TILE // HD):
                at = (t * (TILE // HD) + i) * (LOG_ROWS // BLOCKS) + slot + j
                logs = jnp.where(lanes == at, log[i * HD : (i + 1) * HD], logs)
    return logs


def pack_logs(logs):
    flat = logs.T[:LOG_ROWS]
    high = flat.astype(jnp.bfloat16)
    return jnp.concatenate([high, (flat - high.astype(jnp.float32)).astype(jnp.bfloat16)], 1)


def unpack_logs(packed):
    parts = packed.astype(jnp.float32)
    flat = parts[:, :HD] + parts[:, HD:]
    return jnp.concatenate([flat, jnp.zeros((HD - LOG_ROWS, HD), jnp.float32)], 0).T


def came(q, first, skip, heads):
    chunk = q[0][:, skip * HD : (skip + heads) * HD]
    if len(q) == 1:
        return chunk
    whole = q[1][:, first * HD : (first + heads) * HD]
    return jnp.where(lax.axis_index("head") == 1, whole, chunk)


def lead_kernel(first, heads, count, *refs):
    q, (k, v, even, odd, out, logs) = refs[:count], refs[count:]

    def store(rows, here, block):
        out[rows, here] = block.astype(out.dtype)

    logs[...] = attend(first, heads, came(q, first, 0, heads), k, v, even, odd, store)


def remote_kernel(first, heads, lead, tail, count, *refs):
    q, (k, v, even, odd, *rest) = refs[:count], refs[count:]
    earlier, (out, *last) = rest[: lead > 0], rest[lead > 0 :]

    def store(rows, here, block):
        start = here.start - (heads - tail) * HD
        if start < 0:
            out[rows, here] = block.astype(out.dtype)
        else:
            last[0][rows, start : start + HD] = block.astype(out.dtype)

    q_here = came(q, first, lead, heads)
    sides = [x.at[:, lead * HD : (lead + heads) * HD] for x in (even, odd)]
    logs = attend(first, heads, q_here, k, v, *sides, store, lead)
    packed = pack_logs(logs + earlier[0][...] if lead else logs)
    out[ROWS:, : 2 * HD] = packed
    if out.shape[1] > 2 * HD:
        out[ROWS:, 2 * HD :] = jnp.zeros((LOG_ROWS, out.shape[1] - 2 * HD), out.dtype)


def local_kernel(splits, q, k, v, *rest):
    sides, out, logs = rest[: -1 - len(splits)], rest[-1 - len(splits)], rest[-len(splits) :]
    first = 0
    for c, heads in enumerate(splits):
        columns = slice(first * HD, (first + heads) * HD)

        def store(rows, here, block, first=first):
            out[rows, first * HD + here.start : first * HD + here.stop] = block

        logs[c][...] = attend(
            first, heads, q.at[:, columns], k, v, sides[2 * c], sides[2 * c + 1], store
        )
        first += heads


def shares_of(logs, theirs):
    place = lax.axis_index("row")
    if len(theirs) == 1:
        there = (None,)
    else:
        there = (place < lax.axis_size("row") - 1, place > 0)
    all_logs = [logs[...]]
    for valid, part in zip(there, theirs):
        got = unpack_logs(part[ROWS:, : 2 * HD])
        all_logs.append(got if valid is None else jnp.where(valid, got, -jnp.inf))
    top = functools.reduce(jnp.maximum, all_logs)
    weights = [jnp.exp2(x - top) for x in all_logs]
    total = functools.reduce(jnp.add, weights)
    return [w / total for w in weights]


def write_columns(first, heads, mixed, out, done, fill):
    copies = []
    for b in range(BLOCKS):
        rows = slice(b * HD, (b + 1) * HD)
        fill(b, rows)
        copies.append(
            pltpu.make_async_copy(
                mixed.at[rows, :],
                out.at[rows, first * HD : (first + heads) * HD],
                done.at[b],
            )
        )
        copies[-1].start()
    return copies


def merge_kernel(first, lead, heads, tail, groups, own, logs, *rest):
    leads, rest = rest[: groups * (lead > 0)], rest[groups * (lead > 0) :]
    theirs, (mixed, done) = rest[:groups], rest[-2:]
    out, *later = rest[-3 - (1 + groups) * (tail > 0) : -2]
    shares = shares_of(logs, theirs)

    def fill(b, rows):
        for j in range(heads):
            here = slice(j * HD, (j + 1) * HD)
            at = b * (LOG_ROWS // BLOCKS) + j
            summed = shares[0][:, at : at + 1] * own[rows, (first + j) * HD : (first + j + 1) * HD]
            parts, start = (leads, j * HD) if j < lead else (theirs, (j - lead) * HD)
            for share, part in zip(shares[1:], parts):
                block = part[rows, start : start + HD].astype(jnp.float32)
                summed = summed + share[:, at : at + 1] * block
            mixed[rows, here] = summed.astype(mixed.dtype)

    copies = write_columns(first, heads, mixed, out, done, fill)
    for b in range(BLOCKS):
        for j in range(tail):
            rows, here = slice(b * HD, (b + 1) * HD), slice(j * HD, (j + 1) * HD)
            at = b * (LOG_ROWS // BLOCKS) + heads + j
            own_at = (first + heads + j) * HD
            later[0][rows, here] = shares[0][:, at : at + 1] * own[rows, own_at : own_at + HD]
            for share, spread in zip(shares[1:], later[1:]):
                spread[rows, here] = jnp.broadcast_to(share[:, at : at + 1], (HD, HD))
    for copy in copies:
        copy.wait()


def finish_kernel(first, heads, groups, scaled, *rest):
    shares, theirs = rest[:groups], rest[groups : 2 * groups]
    out, mixed, done = rest[-3:]

    def fill(b, rows):
        summed = scaled[rows, :]
        for share, part in zip(shares, theirs):
            summed = summed + share[rows, :] * part[rows, :].astype(jnp.float32)
        mixed[rows, :] = summed.astype(mixed.dtype)

    for copy in write_columns(first, heads, mixed, out, done, fill):
        copy.wait()


def cost(heads, tiles=6):
    pairs = heads * tiles * TILE * TILE
    return pl.CostEstimate(
        flops=4 * pairs * HD, bytes_accessed=heads * 8 * ROWS * HD, transcendentals=pairs
    )


def in_vmem():
    return pl.BlockSpec(memory_space=pltpu.VMEM)


def lead_part(first, heads, q, k, v, even, odd):
    return pl.pallas_call(
        functools.partial(lead_kernel, first, heads, len(q)),
        in_specs=[in_vmem()] * (4 + len(q)),
        out_specs=[in_vmem()] * 2,
        out_shape=[
            jax.ShapeDtypeStruct((ROWS, heads * HD), jnp.bfloat16),
            jax.ShapeDtypeStruct((HD, HD), jnp.float32),
        ],
        compiler_params=pltpu.CompilerParams(vmem_limit_bytes=VMEM_BYTES),
        cost_estimate=cost(heads),
        name="lead_part",
    )(*q, k, v, even, odd)


def remote_part(first, heads, lead, tail, q, k, v, even, odd, *earlier):
    shapes = [(ROWS + LOG_ROWS, (heads - tail) * HD)] + [(ROWS, tail * HD)] * (tail > 0)
    return pl.pallas_call(
        functools.partial(remote_kernel, first, heads, lead, tail, len(q)),
        in_specs=[in_vmem()] * (4 + len(q) + len(earlier)),
        out_specs=[in_vmem()] * len(shapes),
        out_shape=[jax.ShapeDtypeStruct(shape, jnp.bfloat16) for shape in shapes],
        compiler_params=pltpu.CompilerParams(vmem_limit_bytes=VMEM_BYTES),
        cost_estimate=cost(heads),
        name="remote_part",
    )(*q, k, v, even, odd, *earlier)


def local_part(splits, q, k, v, sides):
    heads = sum(splits)
    return pl.pallas_call(
        functools.partial(local_kernel, splits),
        in_specs=[in_vmem()] * (3 + len(sides)),
        out_specs=[in_vmem()] * (1 + len(splits)),
        out_shape=[
            jax.ShapeDtypeStruct((ROWS, heads * HD), jnp.float32),
            *[jax.ShapeDtypeStruct((HD, HD), jnp.float32) for _ in splits],
        ],
        compiler_params=pltpu.CompilerParams(vmem_limit_bytes=VMEM_BYTES),
        cost_estimate=cost(heads),
        name="local_part",
    )(q, k, v, *sides)


def merge_cost(heads):
    return pl.CostEstimate(
        flops=4 * heads * ROWS * HD, bytes_accessed=heads * 8 * ROWS * HD, transcendentals=0
    )


def copy_scratch(heads):
    return [pltpu.VMEM((ROWS, heads * HD), jnp.bfloat16), pltpu.SemaphoreType.DMA((BLOCKS,))]


def merge_part(first, lead, heads, tail, own, logs, leads, theirs, prior):
    groups = len(theirs)
    count = len(leads) + groups
    later = [jax.ShapeDtypeStruct((ROWS, tail * HD), jnp.float32)] * ((1 + groups) * (tail > 0))
    out, *later = pl.pallas_call(
        functools.partial(merge_kernel, first, lead, heads, tail, groups),
        in_specs=[in_vmem()] * (2 + count) + [pl.BlockSpec(memory_space=pl.ANY)] * len(prior),
        out_specs=[pl.BlockSpec(memory_space=pl.ANY)] + [in_vmem()] * len(later),
        out_shape=[jax.ShapeDtypeStruct(own.shape, jnp.bfloat16)] + later,
        scratch_shapes=copy_scratch(heads),
        input_output_aliases={2 + count: 0} if prior else {},
        compiler_params=pltpu.CompilerParams(vmem_limit_bytes=VMEM_BYTES),
        cost_estimate=merge_cost(heads + tail),
        name="merge_part",
    )(own, logs, *leads, *theirs, *prior)
    return out, later


def finish_part(first, heads, scaled, shares, theirs, out):
    groups = len(theirs)
    return pl.pallas_call(
        functools.partial(finish_kernel, first, heads, groups),
        in_specs=[in_vmem()] * (1 + 2 * groups) + [pl.BlockSpec(memory_space=pl.ANY)],
        out_specs=pl.BlockSpec(memory_space=pl.ANY),
        out_shape=jax.ShapeDtypeStruct(out.shape, out.dtype),
        scratch_shapes=copy_scratch(heads),
        input_output_aliases={1 + 2 * groups: 0},
        compiler_params=pltpu.CompilerParams(vmem_limit_bytes=VMEM_BYTES),
        cost_estimate=merge_cost(heads),
        name="finish_part",
    )(scaled, *shares, *theirs, out)


def frame_pairs(first, frames, cores):
    partner = {}
    for i in range(first, frames - 1, 2):
        partner[i], partner[i + 1] = i + 1, i
    return [
        (i * cores + c, partner[i] * cores + c if i in partner else i * cores + cores - 1 - c)
        for i in range(frames)
        for c in range(cores)
    ]


def per_device(query, keys, values):
    features = query.shape[3]
    heads = features // HD
    splits = CHUNKS
    assert sum(splits) == heads
    q = query.reshape(ROWS, features)
    k = keys.reshape(ROWS, features)
    v = values.reshape(ROWS, features)
    frames = lax.axis_size("frame")
    rows = lax.axis_size("row")
    pairs = [frame_pairs(first, frames, lax.axis_size("head")) for first in (0, 1)]
    place = lax.axis_index("frame")
    if rows == 2:
        routes = [([(0, 1), (1, 0)], [(0, 1), (1, 0)])]
    else:
        down = [(i, i + 1) for i in range(rows - 1)]
        up = [(i + 1, i) for i in range(rows - 1)]
        routes = [(down, up), (up, down)]

    bounds, start = [], 0
    for count in splits:
        bounds.append((start, start + count))
        start += count

    axes = ("clips", "row", "head")
    by_core = [lax.axis_size(axis) for axis in axes] == [2, 2, 2]
    if by_core:
        whole = lax.ppermute(q, axes, ONE_ALONG_X)
    got_q, sides = [], []
    q_now, gate = q, ()
    for a, b in bounds:
        a, b = a * HD, b * HD
        if not by_core:
            sent = q_now[:, a:b]
            got_q.append([(lax.ppermute(sent, "row", there),) for there, _ in routes])
            gate = (gate, sent)
        k_now, v_now, _ = lax.optimization_barrier((k, v, gate))
        halves = []
        for first in (0, 1):
            if first and by_core and sides:
                k_now, v_now, _ = lax.optimization_barrier((k, v, (halves, sides[0][0])))
            row = jnp.where(lax.rem(place, 2) == first, TILE, 0)
            half = [lax.dynamic_slice(x, (row, a), (TILE, b - a)) for x in (k_now, v_now)]
            halves.append(jnp.concatenate(half, 0))
        sides.append([lax.ppermute(h, ("frame", "head"), p) for h, p in zip(halves, pairs)])
        q_now, _ = lax.optimization_barrier((q, halves))
        if not by_core:
            gate = [one[0] for one in got_q[-1]]
        elif not got_q:
            for c, d in bounds:
                sent = q_now[:, c * HD : d * HD]
                got_q.append([(lax.ppermute(sent, axes, ZERO_ALONG_X), whole)])
                q_now, _ = lax.optimization_barrier((q, sent))
            gate = (whole, sent)

    back = [route for _, route in routes]

    def send_back(parts):
        return [lax.ppermute(x, "row", p) for x, p in zip(parts, back)]

    answers, led = [], []
    k_now, v_now = k, v
    for (a, b), lead, tail, chunk_q, (even, odd) in zip(bounds, LEADS, TAILS, got_q, sides):
        parts, firsts = [], []
        for one in chunk_q:
            operands, earlier = (one, k_now, v_now, even, odd), ()
            if lead:
                block, *earlier = lead_part(a, lead, *operands)
                firsts.append(block)
                k_now, v_now, _ = lax.optimization_barrier((k, v, block))
                operands = (one, k_now, v_now, even, odd)
            parts.append(remote_part(a + lead, b - a - lead, lead, tail, *operands, *earlier))
        led.append(send_back(firsts))
        answers.append([list(x) for x in zip(*parts)])
        k_now, v_now, _ = lax.optimization_barrier((k, v, (parts, led[-1])))

    q_local, _ = lax.optimization_barrier((q, answers))
    own, *logs = local_part(splits, q_local, k, v, [s for pair in sides for s in pair])
    out = ()
    for (a, b), lead, tail, log, leads, parts in zip(bounds, LEADS, TAILS, logs, led, answers):
        theirs = send_back(parts[0])
        out, later = merge_part(a, lead, b - a - tail, tail, own, log, leads, theirs, out)
        if tail:
            last, _ = lax.optimization_barrier((parts[1], log))
            out = finish_part(b - tail, tail, later[0], later[1:], send_back(last), out)
        out = (out,)
    (out,) = out
    return out.reshape(query.shape)


def solution(mesh):
    spec = P(("clips", "frame"), "row", None, "head")
    return jax.shard_map(
        per_device, mesh=mesh, in_specs=(spec,) * 3, out_specs=spec, check_vma=False
    )
```

```python
import functools
import math

import jax
import jax.numpy as jnp
from jax import lax
from jax.experimental import pallas as pl
from jax.experimental.pallas import tpu as pltpu
from jax.sharding import PartitionSpec as P

HD = 128
TF = 4
TR = 8
TC = 8
TILE = TF * TR * TC
ROWS = 2 * TILE
EXPONENT = math.log2(math.e) / math.sqrt(HD)
NT = (((1,), (1,)), ((), ()))
NN = (((1,), (0,)), ((), ()))
BLOCKS = ROWS // HD
LOG_ROWS = 16
CHUNKS = (3, 3)
LEADS = (1, 0)
TAILS = (0, 1)
ONE_ALONG_X = tuple((i, i ^ 2 if i % 2 else i ^ 4) for i in range(8))
ZERO_ALONG_X = tuple((i, i ^ 2) for i in range(0, 8, 2))
VMEM_BYTES = 48 * 1024 * 1024


def dot(a, b, dims):
    return lax.dot_general(a, b, dims, preferred_element_type=jnp.float32)


def attend(first, heads, q, k, v, even, odd, store, slot=0):
    place = lax.axis_index("frame")
    present = (place > 0, place < lax.axis_size("frame") - 1)
    is_even = lax.rem(place, 2) == 0
    ones = jnp.ones((ROWS, HD), jnp.bfloat16)
    lanes = lax.broadcasted_iota(jnp.int32, (HD, HD), 1)
    logs = jnp.zeros((HD, HD), jnp.float32)
    for t in range(2):
        rows = slice(t * TILE, (t + 1) * TILE)
        near, far = (odd, even) if t == 0 else (even, odd)
        for j in range(heads):
            here = slice(j * HD, (j + 1) * HD)
            own = slice((first + j) * HD, (first + j + 1) * HD)
            q_tile = q[rows, here]
            k_own = k[:, own]
            v_own = jnp.concatenate([v[:, own], ones], 1)
            side = jnp.where(is_even, near[:, here], far[:, here])
            k_side = jnp.where(present[t], side[:TILE], k_own[:TILE])
            v_side = jnp.concatenate([side[TILE:], ones[:TILE]], 1)
            v_side = jnp.where(present[t], v_side, jnp.zeros_like(v_side))
            s_own = dot(q_tile, k_own, NT)
            s_side = dot(q_tile, k_side, NT)
            peak = jnp.maximum(
                jnp.max(s_own, axis=1, keepdims=True), jnp.max(s_side, axis=1, keepdims=True)
            )
            w_own = jnp.exp2((s_own - peak) * EXPONENT).astype(jnp.bfloat16)
            w_side = jnp.exp2((s_side - peak) * EXPONENT).astype(jnp.bfloat16)
            summed = dot(w_own, v_own, NN) + dot(w_side, v_side, NN)
            total = summed[:, HD:]
            store(rows, here, summed[:, :HD] / total)
            log = peak * EXPONENT + jnp.log2(total[:, :1])
            for i in range(TILE // HD):
                at = (t * (TILE // HD) + i) * (LOG_ROWS // BLOCKS) + slot + j
                logs = jnp.where(lanes == at, log[i * HD : (i + 1) * HD], logs)
    return logs


def pack_logs(logs):
    flat = logs.T[:LOG_ROWS]
    high = flat.astype(jnp.bfloat16)
    return jnp.concatenate([high, (flat - high.astype(jnp.float32)).astype(jnp.bfloat16)], 1)


def unpack_logs(packed):
    parts = packed.astype(jnp.float32)
    flat = parts[:, :HD] + parts[:, HD:]
    return jnp.concatenate([flat, jnp.zeros((HD - LOG_ROWS, HD), jnp.float32)], 0).T


def came(q, first, skip, heads):
    chunk = q[0][:, skip * HD : (skip + heads) * HD]
    if len(q) == 1:
        return chunk
    whole = q[1][:, first * HD : (first + heads) * HD]
    return jnp.where(lax.axis_index("head") == 1, whole, chunk)


def lead_kernel(first, heads, count, *refs):
    q, (k, v, even, odd, out, logs) = refs[:count], refs[count:]

    def store(rows, here, block):
        out[rows, here] = block.astype(out.dtype)

    logs[...] = attend(first, heads, came(q, first, 0, heads), k, v, even, odd, store)


def remote_kernel(first, heads, lead, tail, count, *refs):
    q, (k, v, even, odd, *rest) = refs[:count], refs[count:]
    earlier, (out, *last) = rest[: lead > 0], rest[lead > 0 :]

    def store(rows, here, block):
        start = here.start - (heads - tail) * HD
        if start < 0:
            out[rows, here] = block.astype(out.dtype)
        else:
            last[0][rows, start : start + HD] = block.astype(out.dtype)

    q_here = came(q, first, lead, heads)
    sides = [x.at[:, lead * HD : (lead + heads) * HD] for x in (even, odd)]
    logs = attend(first, heads, q_here, k, v, *sides, store, lead)
    packed = pack_logs(logs + earlier[0][...] if lead else logs)
    out[ROWS:, : 2 * HD] = packed
    if out.shape[1] > 2 * HD:
        out[ROWS:, 2 * HD :] = jnp.zeros((LOG_ROWS, out.shape[1] - 2 * HD), out.dtype)


def local_kernel(splits, q, k, v, *rest):
    sides, out, logs = rest[: -1 - len(splits)], rest[-1 - len(splits)], rest[-len(splits) :]
    first = 0
    for c, heads in enumerate(splits):
        columns = slice(first * HD, (first + heads) * HD)

        def store(rows, here, block, first=first):
            out[rows, first * HD + here.start : first * HD + here.stop] = block

        logs[c][...] = attend(
            first, heads, q.at[:, columns], k, v, sides[2 * c], sides[2 * c + 1], store
        )
        first += heads


def shares_of(logs, theirs):
    place = lax.axis_index("row")
    if len(theirs) == 1:
        there = (None,)
    else:
        there = (place < lax.axis_size("row") - 1, place > 0)
    all_logs = [logs[...]]
    for valid, part in zip(there, theirs):
        got = unpack_logs(part[ROWS:, : 2 * HD])
        all_logs.append(got if valid is None else jnp.where(valid, got, -jnp.inf))
    top = functools.reduce(jnp.maximum, all_logs)
    weights = [jnp.exp2(x - top) for x in all_logs]
    total = functools.reduce(jnp.add, weights)
    return [w / total for w in weights]


def write_columns(first, heads, mixed, out, done, fill):
    copies = []
    for b in range(BLOCKS):
        rows = slice(b * HD, (b + 1) * HD)
        fill(b, rows)
        copies.append(
            pltpu.make_async_copy(
                mixed.at[rows, :],
                out.at[rows, first * HD : (first + heads) * HD],
                done.at[b],
            )
        )
        copies[-1].start()
    return copies


def merge_kernel(first, lead, heads, tail, groups, own, logs, *rest):
    leads, rest = rest[: groups * (lead > 0)], rest[groups * (lead > 0) :]
    theirs, (mixed, done) = rest[:groups], rest[-2:]
    out, *later = rest[-3 - (1 + groups) * (tail > 0) : -2]
    shares = shares_of(logs, theirs)

    def fill(b, rows):
        for j in range(heads):
            here = slice(j * HD, (j + 1) * HD)
            at = b * (LOG_ROWS // BLOCKS) + j
            summed = shares[0][:, at : at + 1] * own[rows, (first + j) * HD : (first + j + 1) * HD]
            parts, start = (leads, j * HD) if j < lead else (theirs, (j - lead) * HD)
            for share, part in zip(shares[1:], parts):
                block = part[rows, start : start + HD].astype(jnp.float32)
                summed = summed + share[:, at : at + 1] * block
            mixed[rows, here] = summed.astype(mixed.dtype)

    copies = write_columns(first, heads, mixed, out, done, fill)
    for b in range(BLOCKS):
        for j in range(tail):
            rows, here = slice(b * HD, (b + 1) * HD), slice(j * HD, (j + 1) * HD)
            at = b * (LOG_ROWS // BLOCKS) + heads + j
            own_at = (first + heads + j) * HD
            later[0][rows, here] = shares[0][:, at : at + 1] * own[rows, own_at : own_at + HD]
            for share, spread in zip(shares[1:], later[1:]):
                spread[rows, here] = jnp.broadcast_to(share[:, at : at + 1], (HD, HD))
    for copy in copies:
        copy.wait()


def finish_kernel(first, heads, groups, scaled, *rest):
    shares, theirs = rest[:groups], rest[groups : 2 * groups]
    out, mixed, done = rest[-3:]

    def fill(b, rows):
        summed = scaled[rows, :]
        for share, part in zip(shares, theirs):
            summed = summed + share[rows, :] * part[rows, :].astype(jnp.float32)
        mixed[rows, :] = summed.astype(mixed.dtype)

    for copy in write_columns(first, heads, mixed, out, done, fill):
        copy.wait()


def cost(heads, tiles=6):
    pairs = heads * tiles * TILE * TILE
    return pl.CostEstimate(
        flops=4 * pairs * HD, bytes_accessed=heads * 8 * ROWS * HD, transcendentals=pairs
    )


def in_vmem():
    return pl.BlockSpec(memory_space=pltpu.VMEM)


def lead_part(first, heads, q, k, v, even, odd):
    return pl.pallas_call(
        functools.partial(lead_kernel, first, heads, len(q)),
        in_specs=[in_vmem()] * (4 + len(q)),
        out_specs=[in_vmem()] * 2,
        out_shape=[
            jax.ShapeDtypeStruct((ROWS, heads * HD), jnp.bfloat16),
            jax.ShapeDtypeStruct((HD, HD), jnp.float32),
        ],
        compiler_params=pltpu.CompilerParams(vmem_limit_bytes=VMEM_BYTES),
        cost_estimate=cost(heads),
        name="lead_part",
    )(*q, k, v, even, odd)


def remote_part(first, heads, lead, tail, q, k, v, even, odd, *earlier):
    shapes = [(ROWS + LOG_ROWS, (heads - tail) * HD)] + [(ROWS, tail * HD)] * (tail > 0)
    return pl.pallas_call(
        functools.partial(remote_kernel, first, heads, lead, tail, len(q)),
        in_specs=[in_vmem()] * (4 + len(q) + len(earlier)),
        out_specs=[in_vmem()] * len(shapes),
        out_shape=[jax.ShapeDtypeStruct(shape, jnp.bfloat16) for shape in shapes],
        compiler_params=pltpu.CompilerParams(vmem_limit_bytes=VMEM_BYTES),
        cost_estimate=cost(heads),
        name="remote_part",
    )(*q, k, v, even, odd, *earlier)


def local_part(splits, q, k, v, sides):
    heads = sum(splits)
    return pl.pallas_call(
        functools.partial(local_kernel, splits),
        in_specs=[in_vmem()] * (3 + len(sides)),
        out_specs=[in_vmem()] * (1 + len(splits)),
        out_shape=[
            jax.ShapeDtypeStruct((ROWS, heads * HD), jnp.float32),
            *[jax.ShapeDtypeStruct((HD, HD), jnp.float32) for _ in splits],
        ],
        compiler_params=pltpu.CompilerParams(vmem_limit_bytes=VMEM_BYTES),
        cost_estimate=cost(heads),
        name="local_part",
    )(q, k, v, *sides)


def merge_cost(heads):
    return pl.CostEstimate(
        flops=4 * heads * ROWS * HD, bytes_accessed=heads * 8 * ROWS * HD, transcendentals=0
    )


def copy_scratch(heads):
    return [pltpu.VMEM((ROWS, heads * HD), jnp.bfloat16), pltpu.SemaphoreType.DMA((BLOCKS,))]


def merge_part(first, lead, heads, tail, own, logs, leads, theirs, prior):
    groups = len(theirs)
    count = len(leads) + groups
    later = [jax.ShapeDtypeStruct((ROWS, tail * HD), jnp.float32)] * ((1 + groups) * (tail > 0))
    out, *later = pl.pallas_call(
        functools.partial(merge_kernel, first, lead, heads, tail, groups),
        in_specs=[in_vmem()] * (2 + count) + [pl.BlockSpec(memory_space=pl.ANY)] * len(prior),
        out_specs=[pl.BlockSpec(memory_space=pl.ANY)] + [in_vmem()] * len(later),
        out_shape=[jax.ShapeDtypeStruct(own.shape, jnp.bfloat16)] + later,
        scratch_shapes=copy_scratch(heads),
        input_output_aliases={2 + count: 0} if prior else {},
        compiler_params=pltpu.CompilerParams(vmem_limit_bytes=VMEM_BYTES),
        cost_estimate=merge_cost(heads + tail),
        name="merge_part",
    )(own, logs, *leads, *theirs, *prior)
    return out, later


def finish_part(first, heads, scaled, shares, theirs, out):
    groups = len(theirs)
    return pl.pallas_call(
        functools.partial(finish_kernel, first, heads, groups),
        in_specs=[in_vmem()] * (1 + 2 * groups) + [pl.BlockSpec(memory_space=pl.ANY)],
        out_specs=pl.BlockSpec(memory_space=pl.ANY),
        out_shape=jax.ShapeDtypeStruct(out.shape, out.dtype),
        scratch_shapes=copy_scratch(heads),
        input_output_aliases={1 + 2 * groups: 0},
        compiler_params=pltpu.CompilerParams(vmem_limit_bytes=VMEM_BYTES),
        cost_estimate=merge_cost(heads),
        name="finish_part",
    )(scaled, *shares, *theirs, out)


def frame_pairs(first, frames, cores):
    partner = {}
    for i in range(first, frames - 1, 2):
        partner[i], partner[i + 1] = i + 1, i
    return [
        (i * cores + c, partner[i] * cores + c if i in partner else i * cores + cores - 1 - c)
        for i in range(frames)
        for c in range(cores)
    ]


def per_device(query, keys, values):
    features = query.shape[3]
    heads = features // HD
    splits = CHUNKS
    assert sum(splits) == heads
    q = query.reshape(ROWS, features)
    k = keys.reshape(ROWS, features)
    v = values.reshape(ROWS, features)
    frames = lax.axis_size("frame")
    rows = lax.axis_size("row")
    pairs = [frame_pairs(first, frames, lax.axis_size("head")) for first in (0, 1)]
    place = lax.axis_index("frame")
    if rows == 2:
        routes = [([(0, 1), (1, 0)], [(0, 1), (1, 0)])]
    else:
        down = [(i, i + 1) for i in range(rows - 1)]
        up = [(i + 1, i) for i in range(rows - 1)]
        routes = [(down, up), (up, down)]

    bounds, start = [], 0
    for count in splits:
        bounds.append((start, start + count))
        start += count

    axes = ("clips", "row", "head")
    by_core = [lax.axis_size(axis) for axis in axes] == [2, 2, 2]
    if by_core:
        whole = lax.ppermute(q, axes, ONE_ALONG_X)
    got_q, sides = [], []
    q_now, gate = q, ()
    for a, b in bounds:
        a, b = a * HD, b * HD
        if not by_core:
            sent = q_now[:, a:b]
            got_q.append([(lax.ppermute(sent, "row", there),) for there, _ in routes])
            gate = (gate, sent)
        k_now, v_now, _ = lax.optimization_barrier((k, v, gate))
        halves = {}
        for first in (1, 0) if by_core and sides else (0, 1):
            if by_core and sides:
                held = (sent, whole) if first else (sent, sides[0][0])
                k_now, v_now, _ = lax.optimization_barrier((k, v, held))
            row = jnp.where(lax.rem(place, 2) == first, TILE, 0)
            half = [lax.dynamic_slice(x, (row, a), (TILE, b - a)) for x in (k_now, v_now)]
            halves[first] = jnp.concatenate(half, 0)
        halves = [halves[0], halves[1]]
        sides.append([lax.ppermute(h, ("frame", "head"), p) for h, p in zip(halves, pairs)])
        q_now, _ = lax.optimization_barrier((q, halves))
        if not by_core:
            gate = [one[0] for one in got_q[-1]]
        elif not got_q:
            for c, d in bounds:
                sent = q_now[:, c * HD : d * HD]
                got_q.append([(lax.ppermute(sent, axes, ZERO_ALONG_X), whole)])
                q_now, _ = lax.optimization_barrier((q, sent))
            gate = (whole, sent)

    back = [route for _, route in routes]

    def send_back(parts):
        return [lax.ppermute(x, "row", p) for x, p in zip(parts, back)]

    answers, led = [], []
    k_now, v_now = k, v
    for (a, b), lead, tail, chunk_q, (even, odd) in zip(bounds, LEADS, TAILS, got_q, sides):
        parts, firsts = [], []
        for one in chunk_q:
            operands, earlier = (one, k_now, v_now, even, odd), ()
            if lead:
                block, *earlier = lead_part(a, lead, *operands)
                firsts.append(block)
                k_now, v_now, _ = lax.optimization_barrier((k, v, block))
                operands = (one, k_now, v_now, even, odd)
            parts.append(remote_part(a + lead, b - a - lead, lead, tail, *operands, *earlier))
        led.append(send_back(firsts))
        answers.append([list(x) for x in zip(*parts)])
        k_now, v_now, _ = lax.optimization_barrier((k, v, (parts, led[-1])))

    q_local, _ = lax.optimization_barrier((q, answers))
    own, *logs = local_part(splits, q_local, k, v, [s for pair in sides for s in pair])
    out = ()
    for (a, b), lead, tail, log, leads, parts in zip(bounds, LEADS, TAILS, logs, led, answers):
        theirs = send_back(parts[0])
        out, later = merge_part(a, lead, b - a - tail, tail, own, log, leads, theirs, out)
        if tail:
            last, _ = lax.optimization_barrier((parts[1], log))
            out = finish_part(b - tail, tail, later[0], later[1:], send_back(last), out)
        out = (out,)
    (out,) = out
    return out.reshape(query.shape)


def solution(mesh):
    spec = P(("clips", "frame"), "row", None, "head")
    return jax.shard_map(
        per_device, mesh=mesh, in_specs=(spec,) * 3, out_specs=spec, check_vma=False
    )
```

```python
import functools
import math

import jax
import jax.numpy as jnp
from jax import lax
from jax.experimental import pallas as pl
from jax.experimental.pallas import tpu as pltpu
from jax.sharding import PartitionSpec as P

HD = 128
TF = 4
TR = 8
TC = 8
TILE = TF * TR * TC
ROWS = 2 * TILE
EXPONENT = math.log2(math.e) / math.sqrt(HD)
NT = (((1,), (1,)), ((), ()))
NN = (((1,), (0,)), ((), ()))
BLOCKS = ROWS // HD
LOG_ROWS = 16
CHUNKS = (3, 3)
LEADS = (0, 0)
TAILS = (0, 1)
ONE_ALONG_X = tuple((i, i ^ 2 if i % 2 else i ^ 4) for i in range(8))
ZERO_ALONG_X = tuple((i, i ^ 2) for i in range(0, 8, 2))
VMEM_BYTES = 48 * 1024 * 1024


def dot(a, b, dims):
    return lax.dot_general(a, b, dims, preferred_element_type=jnp.float32)


def attend(first, heads, q, k, v, even, odd, store, slot=0):
    place = lax.axis_index("frame")
    present = (place > 0, place < lax.axis_size("frame") - 1)
    is_even = lax.rem(place, 2) == 0
    ones = jnp.ones((ROWS, HD), jnp.bfloat16)
    lanes = lax.broadcasted_iota(jnp.int32, (HD, HD), 1)
    logs = jnp.zeros((HD, HD), jnp.float32)
    for t in range(2):
        rows = slice(t * TILE, (t + 1) * TILE)
        near, far = (odd, even) if t == 0 else (even, odd)
        for j in range(heads):
            here = slice(j * HD, (j + 1) * HD)
            own = slice((first + j) * HD, (first + j + 1) * HD)
            q_tile = q[rows, here]
            k_own = k[:, own]
            v_own = jnp.concatenate([v[:, own], ones], 1)
            side = jnp.where(is_even, near[:, here], far[:, here])
            k_side = jnp.where(present[t], side[:TILE], k_own[:TILE])
            v_side = jnp.concatenate([side[TILE:], ones[:TILE]], 1)
            v_side = jnp.where(present[t], v_side, jnp.zeros_like(v_side))
            s_own = dot(q_tile, k_own, NT)
            s_side = dot(q_tile, k_side, NT)
            peak = jnp.maximum(
                jnp.max(s_own, axis=1, keepdims=True), jnp.max(s_side, axis=1, keepdims=True)
            )
            w_own = jnp.exp2((s_own - peak) * EXPONENT).astype(jnp.bfloat16)
            w_side = jnp.exp2((s_side - peak) * EXPONENT).astype(jnp.bfloat16)
            summed = dot(w_own, v_own, NN) + dot(w_side, v_side, NN)
            total = summed[:, HD:]
            store(rows, here, summed[:, :HD] / total)
            log = peak * EXPONENT + jnp.log2(total[:, :1])
            for i in range(TILE // HD):
                at = (t * (TILE // HD) + i) * (LOG_ROWS // BLOCKS) + slot + j
                logs = jnp.where(lanes == at, log[i * HD : (i + 1) * HD], logs)
    return logs


def pack_logs(logs):
    flat = logs.T[:LOG_ROWS]
    high = flat.astype(jnp.bfloat16)
    return jnp.concatenate([high, (flat - high.astype(jnp.float32)).astype(jnp.bfloat16)], 1)


def unpack_logs(packed):
    parts = packed.astype(jnp.float32)
    flat = parts[:, :HD] + parts[:, HD:]
    return jnp.concatenate([flat, jnp.zeros((HD - LOG_ROWS, HD), jnp.float32)], 0).T


def came(q, first, skip, heads):
    chunk = q[0][:, skip * HD : (skip + heads) * HD]
    if len(q) == 1:
        return chunk
    whole = q[1][:, first * HD : (first + heads) * HD]
    return jnp.where(lax.axis_index("head") == 1, whole, chunk)


def lead_kernel(first, heads, count, *refs):
    q, (k, v, even, odd, out, logs) = refs[:count], refs[count:]

    def store(rows, here, block):
        out[rows, here] = block.astype(out.dtype)

    logs[...] = attend(first, heads, came(q, first, 0, heads), k, v, even, odd, store)


def remote_kernel(first, heads, lead, tail, count, *refs):
    q, (k, v, even, odd, *rest) = refs[:count], refs[count:]
    earlier, (out, *last) = rest[: lead > 0], rest[lead > 0 :]

    def store(rows, here, block):
        start = here.start - (heads - tail) * HD
        if start < 0:
            out[rows, here] = block.astype(out.dtype)
        else:
            last[0][rows, start : start + HD] = block.astype(out.dtype)

    q_here = came(q, first, lead, heads)
    sides = [x.at[:, lead * HD : (lead + heads) * HD] for x in (even, odd)]
    logs = attend(first, heads, q_here, k, v, *sides, store, lead)
    packed = pack_logs(logs + earlier[0][...] if lead else logs)
    out[ROWS:, : 2 * HD] = packed
    if out.shape[1] > 2 * HD:
        out[ROWS:, 2 * HD :] = jnp.zeros((LOG_ROWS, out.shape[1] - 2 * HD), out.dtype)


def local_kernel(splits, q, k, v, *rest):
    sides, out, logs = rest[: -1 - len(splits)], rest[-1 - len(splits)], rest[-len(splits) :]
    first = 0
    for c, heads in enumerate(splits):
        columns = slice(first * HD, (first + heads) * HD)

        def store(rows, here, block, first=first):
            out[rows, first * HD + here.start : first * HD + here.stop] = block

        logs[c][...] = attend(
            first, heads, q.at[:, columns], k, v, sides[2 * c], sides[2 * c + 1], store
        )
        first += heads


def shares_of(logs, theirs):
    place = lax.axis_index("row")
    if len(theirs) == 1:
        there = (None,)
    else:
        there = (place < lax.axis_size("row") - 1, place > 0)
    all_logs = [logs[...]]
    for valid, part in zip(there, theirs):
        got = unpack_logs(part[ROWS:, : 2 * HD])
        all_logs.append(got if valid is None else jnp.where(valid, got, -jnp.inf))
    top = functools.reduce(jnp.maximum, all_logs)
    weights = [jnp.exp2(x - top) for x in all_logs]
    total = functools.reduce(jnp.add, weights)
    return [w / total for w in weights]


def write_columns(first, heads, mixed, out, done, fill):
    copies = []
    for b in range(BLOCKS):
        rows = slice(b * HD, (b + 1) * HD)
        fill(b, rows)
        copies.append(
            pltpu.make_async_copy(
                mixed.at[rows, :],
                out.at[rows, first * HD : (first + heads) * HD],
                done.at[b],
            )
        )
        copies[-1].start()
    return copies


def merge_kernel(first, lead, heads, tail, groups, own, logs, *rest):
    leads, rest = rest[: groups * (lead > 0)], rest[groups * (lead > 0) :]
    theirs, (mixed, done) = rest[:groups], rest[-2:]
    out, *later = rest[-3 - (1 + groups) * (tail > 0) : -2]
    shares = shares_of(logs, theirs)

    def fill(b, rows):
        for j in range(heads):
            here = slice(j * HD, (j + 1) * HD)
            at = b * (LOG_ROWS // BLOCKS) + j
            summed = shares[0][:, at : at + 1] * own[rows, (first + j) * HD : (first + j + 1) * HD]
            parts, start = (leads, j * HD) if j < lead else (theirs, (j - lead) * HD)
            for share, part in zip(shares[1:], parts):
                block = part[rows, start : start + HD].astype(jnp.float32)
                summed = summed + share[:, at : at + 1] * block
            mixed[rows, here] = summed.astype(mixed.dtype)

    copies = write_columns(first, heads, mixed, out, done, fill)
    for b in range(BLOCKS):
        for j in range(tail):
            rows, here = slice(b * HD, (b + 1) * HD), slice(j * HD, (j + 1) * HD)
            at = b * (LOG_ROWS // BLOCKS) + heads + j
            own_at = (first + heads + j) * HD
            later[0][rows, here] = shares[0][:, at : at + 1] * own[rows, own_at : own_at + HD]
            for share, spread in zip(shares[1:], later[1:]):
                spread[rows, here] = jnp.broadcast_to(share[:, at : at + 1], (HD, HD))
    for copy in copies:
        copy.wait()


def finish_kernel(first, heads, groups, scaled, *rest):
    shares, theirs = rest[:groups], rest[groups : 2 * groups]
    out, mixed, done = rest[-3:]

    def fill(b, rows):
        summed = scaled[rows, :]
        for share, part in zip(shares, theirs):
            summed = summed + share[rows, :] * part[rows, :].astype(jnp.float32)
        mixed[rows, :] = summed.astype(mixed.dtype)

    for copy in write_columns(first, heads, mixed, out, done, fill):
        copy.wait()


def cost(heads, tiles=6):
    pairs = heads * tiles * TILE * TILE
    return pl.CostEstimate(
        flops=4 * pairs * HD, bytes_accessed=heads * 8 * ROWS * HD, transcendentals=pairs
    )


def in_vmem():
    return pl.BlockSpec(memory_space=pltpu.VMEM)


def lead_part(first, heads, q, k, v, even, odd):
    return pl.pallas_call(
        functools.partial(lead_kernel, first, heads, len(q)),
        in_specs=[in_vmem()] * (4 + len(q)),
        out_specs=[in_vmem()] * 2,
        out_shape=[
            jax.ShapeDtypeStruct((ROWS, heads * HD), jnp.bfloat16),
            jax.ShapeDtypeStruct((HD, HD), jnp.float32),
        ],
        compiler_params=pltpu.CompilerParams(vmem_limit_bytes=VMEM_BYTES),
        cost_estimate=cost(heads),
        name="lead_part",
    )(*q, k, v, even, odd)


def remote_part(first, heads, lead, tail, q, k, v, even, odd, *earlier):
    shapes = [(ROWS + LOG_ROWS, (heads - tail) * HD)] + [(ROWS, tail * HD)] * (tail > 0)
    return pl.pallas_call(
        functools.partial(remote_kernel, first, heads, lead, tail, len(q)),
        in_specs=[in_vmem()] * (4 + len(q) + len(earlier)),
        out_specs=[in_vmem()] * len(shapes),
        out_shape=[jax.ShapeDtypeStruct(shape, jnp.bfloat16) for shape in shapes],
        compiler_params=pltpu.CompilerParams(vmem_limit_bytes=VMEM_BYTES),
        cost_estimate=cost(heads),
        name="remote_part",
    )(*q, k, v, even, odd, *earlier)


def local_part(splits, q, k, v, sides):
    heads = sum(splits)
    return pl.pallas_call(
        functools.partial(local_kernel, splits),
        in_specs=[in_vmem()] * (3 + len(sides)),
        out_specs=[in_vmem()] * (1 + len(splits)),
        out_shape=[
            jax.ShapeDtypeStruct((ROWS, heads * HD), jnp.float32),
            *[jax.ShapeDtypeStruct((HD, HD), jnp.float32) for _ in splits],
        ],
        compiler_params=pltpu.CompilerParams(vmem_limit_bytes=VMEM_BYTES),
        cost_estimate=cost(heads),
        name="local_part",
    )(q, k, v, *sides)


def merge_cost(heads):
    return pl.CostEstimate(
        flops=4 * heads * ROWS * HD, bytes_accessed=heads * 8 * ROWS * HD, transcendentals=0
    )


def copy_scratch(heads):
    return [pltpu.VMEM((ROWS, heads * HD), jnp.bfloat16), pltpu.SemaphoreType.DMA((BLOCKS,))]


def merge_part(first, lead, heads, tail, own, logs, leads, theirs, prior):
    groups = len(theirs)
    count = len(leads) + groups
    later = [jax.ShapeDtypeStruct((ROWS, tail * HD), jnp.float32)] * ((1 + groups) * (tail > 0))
    out, *later = pl.pallas_call(
        functools.partial(merge_kernel, first, lead, heads, tail, groups),
        in_specs=[in_vmem()] * (2 + count) + [pl.BlockSpec(memory_space=pl.ANY)] * len(prior),
        out_specs=[pl.BlockSpec(memory_space=pl.ANY)] + [in_vmem()] * len(later),
        out_shape=[jax.ShapeDtypeStruct(own.shape, jnp.bfloat16)] + later,
        scratch_shapes=copy_scratch(heads),
        input_output_aliases={2 + count: 0} if prior else {},
        compiler_params=pltpu.CompilerParams(vmem_limit_bytes=VMEM_BYTES),
        cost_estimate=merge_cost(heads + tail),
        name="merge_part",
    )(own, logs, *leads, *theirs, *prior)
    return out, later


def finish_part(first, heads, scaled, shares, theirs, out):
    groups = len(theirs)
    return pl.pallas_call(
        functools.partial(finish_kernel, first, heads, groups),
        in_specs=[in_vmem()] * (1 + 2 * groups) + [pl.BlockSpec(memory_space=pl.ANY)],
        out_specs=pl.BlockSpec(memory_space=pl.ANY),
        out_shape=jax.ShapeDtypeStruct(out.shape, out.dtype),
        scratch_shapes=copy_scratch(heads),
        input_output_aliases={1 + 2 * groups: 0},
        compiler_params=pltpu.CompilerParams(vmem_limit_bytes=VMEM_BYTES),
        cost_estimate=merge_cost(heads),
        name="finish_part",
    )(scaled, *shares, *theirs, out)


def frame_pairs(first, frames, cores):
    partner = {}
    for i in range(first, frames - 1, 2):
        partner[i], partner[i + 1] = i + 1, i
    return [
        (i * cores + c, partner[i] * cores + c if i in partner else i * cores + cores - 1 - c)
        for i in range(frames)
        for c in range(cores)
    ]


def per_device(query, keys, values):
    features = query.shape[3]
    heads = features // HD
    splits = CHUNKS
    assert sum(splits) == heads
    q = query.reshape(ROWS, features)
    k = keys.reshape(ROWS, features)
    v = values.reshape(ROWS, features)
    frames = lax.axis_size("frame")
    rows = lax.axis_size("row")
    pairs = [frame_pairs(first, frames, lax.axis_size("head")) for first in (0, 1)]
    place = lax.axis_index("frame")
    if rows == 2:
        routes = [([(0, 1), (1, 0)], [(0, 1), (1, 0)])]
    else:
        down = [(i, i + 1) for i in range(rows - 1)]
        up = [(i + 1, i) for i in range(rows - 1)]
        routes = [(down, up), (up, down)]

    bounds, start = [], 0
    for count in splits:
        bounds.append((start, start + count))
        start += count

    axes = ("clips", "row", "head")
    by_core = [lax.axis_size(axis) for axis in axes] == [2, 2, 2]
    if by_core:
        whole = lax.ppermute(q, axes, ONE_ALONG_X)
    got_q, sides = [], []
    q_now, gate = q, ()
    for a, b in bounds:
        a, b = a * HD, b * HD
        if not by_core:
            sent = q_now[:, a:b]
            got_q.append([(lax.ppermute(sent, "row", there),) for there, _ in routes])
            gate = (gate, sent)
        k_now, v_now, _ = lax.optimization_barrier((k, v, gate))
        halves = {}
        for first in (0, 1) if by_core and sides else (0, 1):
            if by_core and sides and halves:
                k_now, v_now, _ = lax.optimization_barrier((k, v, (halves, whole)))
            row = jnp.where(lax.rem(place, 2) == first, TILE, 0)
            half = [lax.dynamic_slice(x, (row, a), (TILE, b - a)) for x in (k_now, v_now)]
            halves[first] = jnp.concatenate(half, 0)
        halves = [halves[0], halves[1]]
        sides.append([lax.ppermute(h, ("frame", "head"), p) for h, p in zip(halves, pairs)])
        q_now, _ = lax.optimization_barrier((q, halves))
        if not by_core:
            gate = [one[0] for one in got_q[-1]]
        elif not got_q:
            for c, d in bounds:
                sent = q_now[:, c * HD : d * HD]
                got_q.append([(lax.ppermute(sent, axes, ZERO_ALONG_X), whole)])
                q_now, _ = lax.optimization_barrier((q, sent))
            gate = (whole, sent)

    back = [route for _, route in routes]

    def send_back(parts):
        return [lax.ppermute(x, "row", p) for x, p in zip(parts, back)]

    answers, led = [], []
    k_now, v_now = k, v
    for (a, b), lead, tail, chunk_q, (even, odd) in zip(bounds, LEADS, TAILS, got_q, sides):
        parts, firsts = [], []
        for one in chunk_q:
            operands, earlier = (one, k_now, v_now, even, odd), ()
            if lead:
                block, *earlier = lead_part(a, lead, *operands)
                firsts.append(block)
                k_now, v_now, _ = lax.optimization_barrier((k, v, block))
                operands = (one, k_now, v_now, even, odd)
            parts.append(remote_part(a + lead, b - a - lead, lead, tail, *operands, *earlier))
        led.append(send_back(firsts))
        answers.append([list(x) for x in zip(*parts)])
        k_now, v_now, _ = lax.optimization_barrier((k, v, (parts, led[-1])))

    q_local, _ = lax.optimization_barrier((q, answers))
    own, *logs = local_part(splits, q_local, k, v, [s for pair in sides for s in pair])
    out = ()
    for (a, b), lead, tail, log, leads, parts in zip(bounds, LEADS, TAILS, logs, led, answers):
        theirs = send_back(parts[0])
        out, later = merge_part(a, lead, b - a - tail, tail, own, log, leads, theirs, out)
        if tail:
            last, _ = lax.optimization_barrier((parts[1], log))
            out = finish_part(b - tail, tail, later[0], later[1:], send_back(last), out)
        out = (out,)
    (out,) = out
    return out.reshape(query.shape)


def solution(mesh):
    spec = P(("clips", "frame"), "row", None, "head")
    return jax.shard_map(
        per_device, mesh=mesh, in_specs=(spec,) * 3, out_specs=spec, check_vma=False
    )
```

```python
import functools
import math

import jax
import jax.numpy as jnp
from jax import lax
from jax.experimental import pallas as pl
from jax.experimental.pallas import tpu as pltpu
from jax.sharding import PartitionSpec as P

HD = 128
TF = 4
TR = 8
TC = 8
TILE = TF * TR * TC
ROWS = 2 * TILE
EXPONENT = math.log2(math.e) / math.sqrt(HD)
NT = (((1,), (1,)), ((), ()))
NN = (((1,), (0,)), ((), ()))
BLOCKS = ROWS // HD
LOG_ROWS = 16
CHUNKS = (3, 3)
LEADS = (1, 0)
TAILS = (0, 1)
ONE_ALONG_X = tuple((i, i ^ 2 if i % 2 else i ^ 4) for i in range(8))
ZERO_ALONG_X = tuple((i, i ^ 2) for i in range(0, 8, 2))
VMEM_BYTES = 48 * 1024 * 1024


def dot(a, b, dims):
    return lax.dot_general(a, b, dims, preferred_element_type=jnp.float32)


def attend(first, heads, q, k, v, even, odd, store, slot=0):
    place = lax.axis_index("frame")
    present = (place > 0, place < lax.axis_size("frame") - 1)
    is_even = lax.rem(place, 2) == 0
    ones = jnp.ones((ROWS, HD), jnp.bfloat16)
    lanes = lax.broadcasted_iota(jnp.int32, (HD, HD), 1)
    logs = jnp.zeros((HD, HD), jnp.float32)
    for t in range(2):
        rows = slice(t * TILE, (t + 1) * TILE)
        near, far = (odd, even) if t == 0 else (even, odd)
        for j in range(heads):
            here = slice(j * HD, (j + 1) * HD)
            own = slice((first + j) * HD, (first + j + 1) * HD)
            q_tile = q[rows, here]
            k_own = k[:, own]
            v_own = jnp.concatenate([v[:, own], ones], 1)
            side = jnp.where(is_even, near[:, here], far[:, here])
            k_side = jnp.where(present[t], side[:TILE], k_own[:TILE])
            v_side = jnp.concatenate([side[TILE:], ones[:TILE]], 1)
            v_side = jnp.where(present[t], v_side, jnp.zeros_like(v_side))
            s_own = dot(q_tile, k_own, NT)
            s_side = dot(q_tile, k_side, NT)
            peak = jnp.maximum(
                jnp.max(s_own, axis=1, keepdims=True), jnp.max(s_side, axis=1, keepdims=True)
            )
            w_own = jnp.exp2((s_own - peak) * EXPONENT).astype(jnp.bfloat16)
            w_side = jnp.exp2((s_side - peak) * EXPONENT).astype(jnp.bfloat16)
            summed = dot(w_own, v_own, NN) + dot(w_side, v_side, NN)
            total = summed[:, HD:]
            store(rows, here, summed[:, :HD] / total)
            log = peak * EXPONENT + jnp.log2(total[:, :1])
            for i in range(TILE // HD):
                at = (t * (TILE // HD) + i) * (LOG_ROWS // BLOCKS) + slot + j
                logs = jnp.where(lanes == at, log[i * HD : (i + 1) * HD], logs)
    return logs


def pack_logs(logs):
    flat = logs.T[:LOG_ROWS]
    high = flat.astype(jnp.bfloat16)
    return jnp.concatenate([high, (flat - high.astype(jnp.float32)).astype(jnp.bfloat16)], 1)


def unpack_logs(packed):
    parts = packed.astype(jnp.float32)
    flat = parts[:, :HD] + parts[:, HD:]
    return jnp.concatenate([flat, jnp.zeros((HD - LOG_ROWS, HD), jnp.float32)], 0).T


def came(q, first, skip, heads):
    chunk = q[0][:, skip * HD : (skip + heads) * HD]
    if len(q) == 1:
        return chunk
    whole = q[1][:, first * HD : (first + heads) * HD]
    return jnp.where(lax.axis_index("head") == 1, whole, chunk)


def lead_kernel(first, heads, count, *refs):
    q, (k, v, even, odd, out, logs) = refs[:count], refs[count:]

    def store(rows, here, block):
        out[rows, here] = block.astype(out.dtype)

    logs[...] = attend(first, heads, came(q, first, 0, heads), k, v, even, odd, store)


def remote_kernel(first, heads, lead, tail, count, *refs):
    q, (k, v, even, odd, *rest) = refs[:count], refs[count:]
    earlier, (out, *last) = rest[: lead > 0], rest[lead > 0 :]

    def store(rows, here, block):
        start = here.start - (heads - tail) * HD
        if start < 0:
            out[rows, here] = block.astype(out.dtype)
        else:
            last[0][rows, start : start + HD] = block.astype(out.dtype)

    q_here = came(q, first, lead, heads)
    sides = [x.at[:, lead * HD : (lead + heads) * HD] for x in (even, odd)]
    logs = attend(first, heads, q_here, k, v, *sides, store, lead)
    packed = pack_logs(logs + earlier[0][...] if lead else logs)
    out[ROWS:, : 2 * HD] = packed
    if out.shape[1] > 2 * HD:
        out[ROWS:, 2 * HD :] = jnp.zeros((LOG_ROWS, out.shape[1] - 2 * HD), out.dtype)


def local_kernel(first, heads, q, k, v, even, odd, out, logs):
    def store(rows, here, block):
        out[rows, here] = block

    mine = q.at[:, first * HD : (first + heads) * HD]
    logs[...] = attend(first, heads, mine, k, v, even, odd, store)


def shares_of(logs, theirs):
    place = lax.axis_index("row")
    if len(theirs) == 1:
        there = (None,)
    else:
        there = (place < lax.axis_size("row") - 1, place > 0)
    all_logs = [logs[...]]
    for valid, part in zip(there, theirs):
        got = unpack_logs(part[ROWS:, : 2 * HD])
        all_logs.append(got if valid is None else jnp.where(valid, got, -jnp.inf))
    top = functools.reduce(jnp.maximum, all_logs)
    weights = [jnp.exp2(x - top) for x in all_logs]
    total = functools.reduce(jnp.add, weights)
    return [w / total for w in weights]


def write_columns(first, heads, mixed, out, done, fill):
    copies = []
    for b in range(BLOCKS):
        rows = slice(b * HD, (b + 1) * HD)
        fill(b, rows)
        copies.append(
            pltpu.make_async_copy(
                mixed.at[rows, :],
                out.at[rows, first * HD : (first + heads) * HD],
                done.at[b],
            )
        )
        copies[-1].start()
    return copies


def merge_kernel(first, lead, heads, tail, groups, own, logs, *rest):
    leads, rest = rest[: groups * (lead > 0)], rest[groups * (lead > 0) :]
    theirs, (mixed, done) = rest[:groups], rest[-2:]
    out, *later = rest[-3 - (1 + groups) * (tail > 0) : -2]
    shares = shares_of(logs, theirs)

    def fill(b, rows):
        for j in range(heads):
            here = slice(j * HD, (j + 1) * HD)
            at = b * (LOG_ROWS // BLOCKS) + j
            summed = shares[0][:, at : at + 1] * own[rows, here]
            parts, start = (leads, j * HD) if j < lead else (theirs, (j - lead) * HD)
            for share, part in zip(shares[1:], parts):
                block = part[rows, start : start + HD].astype(jnp.float32)
                summed = summed + share[:, at : at + 1] * block
            mixed[rows, here] = summed.astype(mixed.dtype)

    copies = write_columns(first, heads, mixed, out, done, fill)
    for b in range(BLOCKS):
        for j in range(tail):
            rows, here = slice(b * HD, (b + 1) * HD), slice(j * HD, (j + 1) * HD)
            at = b * (LOG_ROWS // BLOCKS) + heads + j
            own_at = (heads + j) * HD
            later[0][rows, here] = shares[0][:, at : at + 1] * own[rows, own_at : own_at + HD]
            for share, spread in zip(shares[1:], later[1:]):
                spread[rows, here] = jnp.broadcast_to(share[:, at : at + 1], (HD, HD))
    for copy in copies:
        copy.wait()


def finish_kernel(first, heads, groups, scaled, *rest):
    shares, theirs = rest[:groups], rest[groups : 2 * groups]
    out, mixed, done = rest[-3:]

    def fill(b, rows):
        summed = scaled[rows, :]
        for share, part in zip(shares, theirs):
            summed = summed + share[rows, :] * part[rows, :].astype(jnp.float32)
        mixed[rows, :] = summed.astype(mixed.dtype)

    for copy in write_columns(first, heads, mixed, out, done, fill):
        copy.wait()


def cost(heads, tiles=6):
    pairs = heads * tiles * TILE * TILE
    return pl.CostEstimate(
        flops=4 * pairs * HD, bytes_accessed=heads * 8 * ROWS * HD, transcendentals=pairs
    )


def in_vmem():
    return pl.BlockSpec(memory_space=pltpu.VMEM)


def lead_part(first, heads, q, k, v, even, odd):
    return pl.pallas_call(
        functools.partial(lead_kernel, first, heads, len(q)),
        in_specs=[in_vmem()] * (4 + len(q)),
        out_specs=[in_vmem()] * 2,
        out_shape=[
            jax.ShapeDtypeStruct((ROWS, heads * HD), jnp.bfloat16),
            jax.ShapeDtypeStruct((HD, HD), jnp.float32),
        ],
        compiler_params=pltpu.CompilerParams(vmem_limit_bytes=VMEM_BYTES),
        cost_estimate=cost(heads),
        name="lead_part",
    )(*q, k, v, even, odd)


def remote_part(first, heads, lead, tail, q, k, v, even, odd, *earlier):
    shapes = [(ROWS + LOG_ROWS, (heads - tail) * HD)] + [(ROWS, tail * HD)] * (tail > 0)
    return pl.pallas_call(
        functools.partial(remote_kernel, first, heads, lead, tail, len(q)),
        in_specs=[in_vmem()] * (4 + len(q) + len(earlier)),
        out_specs=[in_vmem()] * len(shapes),
        out_shape=[jax.ShapeDtypeStruct(shape, jnp.bfloat16) for shape in shapes],
        compiler_params=pltpu.CompilerParams(vmem_limit_bytes=VMEM_BYTES),
        cost_estimate=cost(heads),
        name="remote_part",
    )(*q, k, v, even, odd, *earlier)


def local_part(first, heads, q, k, v, even, odd):
    return pl.pallas_call(
        functools.partial(local_kernel, first, heads),
        in_specs=[in_vmem()] * 5,
        out_specs=[in_vmem()] * 2,
        out_shape=[
            jax.ShapeDtypeStruct((ROWS, heads * HD), jnp.float32),
            jax.ShapeDtypeStruct((HD, HD), jnp.float32),
        ],
        compiler_params=pltpu.CompilerParams(vmem_limit_bytes=VMEM_BYTES),
        cost_estimate=cost(heads),
        name="local_part",
    )(q, k, v, even, odd)


def merge_cost(heads):
    return pl.CostEstimate(
        flops=4 * heads * ROWS * HD, bytes_accessed=heads * 8 * ROWS * HD, transcendentals=0
    )


def copy_scratch(heads):
    return [pltpu.VMEM((ROWS, heads * HD), jnp.bfloat16), pltpu.SemaphoreType.DMA((BLOCKS,))]


def merge_part(first, lead, heads, tail, width, own, logs, leads, theirs, prior):
    groups = len(theirs)
    count = len(leads) + groups
    later = [jax.ShapeDtypeStruct((ROWS, tail * HD), jnp.float32)] * ((1 + groups) * (tail > 0))
    out, *later = pl.pallas_call(
        functools.partial(merge_kernel, first, lead, heads, tail, groups),
        in_specs=[in_vmem()] * (2 + count) + [pl.BlockSpec(memory_space=pl.ANY)] * len(prior),
        out_specs=[pl.BlockSpec(memory_space=pl.ANY)] + [in_vmem()] * len(later),
        out_shape=[jax.ShapeDtypeStruct((ROWS, width), jnp.bfloat16)] + later,
        scratch_shapes=copy_scratch(heads),
        input_output_aliases={2 + count: 0} if prior else {},
        compiler_params=pltpu.CompilerParams(vmem_limit_bytes=VMEM_BYTES),
        cost_estimate=merge_cost(heads + tail),
        name="merge_part",
    )(own, logs, *leads, *theirs, *prior)
    return out, later


def finish_part(first, heads, scaled, shares, theirs, out):
    groups = len(theirs)
    return pl.pallas_call(
        functools.partial(finish_kernel, first, heads, groups),
        in_specs=[in_vmem()] * (1 + 2 * groups) + [pl.BlockSpec(memory_space=pl.ANY)],
        out_specs=pl.BlockSpec(memory_space=pl.ANY),
        out_shape=jax.ShapeDtypeStruct(out.shape, out.dtype),
        scratch_shapes=copy_scratch(heads),
        input_output_aliases={1 + 2 * groups: 0},
        compiler_params=pltpu.CompilerParams(vmem_limit_bytes=VMEM_BYTES),
        cost_estimate=merge_cost(heads),
        name="finish_part",
    )(scaled, *shares, *theirs, out)


def frame_pairs(first, frames, cores):
    partner = {}
    for i in range(first, frames - 1, 2):
        partner[i], partner[i + 1] = i + 1, i
    return [
        (i * cores + c, partner[i] * cores + c if i in partner else i * cores + cores - 1 - c)
        for i in range(frames)
        for c in range(cores)
    ]


def per_device(query, keys, values):
    features = query.shape[3]
    heads = features // HD
    splits = CHUNKS
    assert sum(splits) == heads
    q = query.reshape(ROWS, features)
    k = keys.reshape(ROWS, features)
    v = values.reshape(ROWS, features)
    frames = lax.axis_size("frame")
    rows = lax.axis_size("row")
    pairs = [frame_pairs(first, frames, lax.axis_size("head")) for first in (0, 1)]
    place = lax.axis_index("frame")
    if rows == 2:
        routes = [([(0, 1), (1, 0)], [(0, 1), (1, 0)])]
    else:
        down = [(i, i + 1) for i in range(rows - 1)]
        up = [(i + 1, i) for i in range(rows - 1)]
        routes = [(down, up), (up, down)]

    bounds, start = [], 0
    for count in splits:
        bounds.append((start, start + count))
        start += count

    axes = ("clips", "row", "head")
    by_core = [lax.axis_size(axis) for axis in axes] == [2, 2, 2]
    if by_core:
        whole = lax.ppermute(q, axes, ONE_ALONG_X)
    got_q, sides = [], []
    q_now, gate = q, ()
    for a, b in bounds:
        a, b = a * HD, b * HD
        if not by_core:
            sent = q_now[:, a:b]
            got_q.append([(lax.ppermute(sent, "row", there),) for there, _ in routes])
            gate = (gate, sent)
        k_now, v_now, _ = lax.optimization_barrier((k, v, gate))
        halves = {}
        for first in (1, 0) if by_core and sides else (0, 1):
            if by_core and sides:
                held = (sent, whole) if first else (sent, sides[0][0])
                k_now, v_now, _ = lax.optimization_barrier((k, v, held))
            row = jnp.where(lax.rem(place, 2) == first, TILE, 0)
            half = [lax.dynamic_slice(x, (row, a), (TILE, b - a)) for x in (k_now, v_now)]
            halves[first] = jnp.concatenate(half, 0)
        halves = [halves[0], halves[1]]
        sides.append([lax.ppermute(h, ("frame", "head"), p) for h, p in zip(halves, pairs)])
        q_now, _ = lax.optimization_barrier((q, halves))
        if not by_core:
            gate = [one[0] for one in got_q[-1]]
        elif not got_q:
            for c, d in bounds:
                sent = q_now[:, c * HD : d * HD]
                got_q.append([(lax.ppermute(sent, axes, ZERO_ALONG_X), whole)])
                q_now, _ = lax.optimization_barrier((q, sent))
            gate = (whole, sent)

    back = [route for _, route in routes]

    def send_back(parts):
        return [lax.ppermute(x, "row", p) for x, p in zip(parts, back)]

    answers, led, kept = [], [], []
    k_now, v_now = k, v
    for (a, b), lead, tail, chunk_q, (even, odd) in zip(bounds, LEADS, TAILS, got_q, sides):
        parts, firsts = [], []
        for one in chunk_q:
            operands, earlier = (one, k_now, v_now, even, odd), ()
            if lead:
                block, *earlier = lead_part(a, lead, *operands)
                firsts.append(block)
                k_now, v_now, _ = lax.optimization_barrier((k, v, block))
                operands = (one, k_now, v_now, even, odd)
            parts.append(remote_part(a + lead, b - a - lead, lead, tail, *operands, *earlier))
        led.append(send_back(firsts))
        answers.append([list(x) for x in zip(*parts)])
        q_now, _ = lax.optimization_barrier((q, parts))
        kept.append(local_part(a, b - a, q_now, k, v, even, odd))
        k_now, v_now, _ = lax.optimization_barrier((k, v, (parts, led[-1], kept[-1][1])))

    out = ()
    for (a, b), lead, tail, (own, log), leads, parts in zip(
        bounds, LEADS, TAILS, kept, led, answers
    ):
        theirs = send_back(parts[0])
        out, later = merge_part(
            a, lead, b - a - tail, tail, features, own, log, leads, theirs, out
        )
        if tail:
            last, _ = lax.optimization_barrier((parts[1], log))
            out = finish_part(b - tail, tail, later[0], later[1:], send_back(last), out)
        out = (out,)
    (out,) = out
    return out.reshape(query.shape)


def solution(mesh):
    spec = P(("clips", "frame"), "row", None, "head")
    return jax.shard_map(
        per_device, mesh=mesh, in_specs=(spec,) * 3, out_specs=spec, check_vma=False
    )
```
